512 devices in a mesh: dp: 64 (over y, z), mp: 8 (over x, core).
Axes of the slice: x: 4, y: 8, z: 8, core: 2. Of those that a mesh axis runs over, the one named last changes fastest.
Arguments:
- context: bfloat16 [12288, 2048], P('dp', 'mp'), may hold values from -8 to 8, as said below
- cotangent: bfloat16 [12288, 4096], P('dp'), may hold values from -8 to 8, as said below
- master_weight: float32 [2048, 4096], P(('mp', 'dp')), may hold values from -0.09375 to 0.09375
- row_state: float32 [2048], P(('mp', 'dp')), may hold values from 0.1 to 1
- col_state: float32 [4096], replicated, may hold values from 0.16666667 to 1.6666666
Outputs:
- grad_input: bfloat16 [12288, 2048], P('dp', 'mp')
- update: float32 [2048, 4096], P(('mp', 'dp'))
- row_new: float32 [2048], P(('mp', 'dp'))
- col_new: float32 [4096], replicated
- update_rms: float32 [], replicated
The draws below stay inside these ranges and needn't reach their ends.
Inputs may be any that keep to these rules, and one draw needn't show every extreme that they name: context values, column scales vary. cotangent values, column scales vary.
All inputs are finite; a program needn't handle non-finite values.
Results may differ from the reference program's by a relative error of at most 0.001.
The reference program's roundings to bfloat16 on the way (of `weight_copy`) count: a program that leaves them out, or rounds other values in their place, can miss the bound.
Values may be sent and summed in bfloat16 or wider, within the bound.
No kernel may reach another device: no remote copies, remote signals or barrier semaphores. Data moves between devices by JAX's collectives and lax.ppermute only.
A program may use at most 64 MiB of HBM per device.

```python
import math
import jax
import jax.numpy as jnp
from jax import lax

D = 4096
HD = 2048
TOKENS = 12288


def scaled_field(key, rows, cols):
    keys = jax.random.split(key, 3)
    col_scale = jnp.exp(jax.random.uniform(keys[0], (cols,), jnp.float32) * math.log(10.0)) / 4.64
    noise = jax.random.normal(keys[2], (rows, cols), jnp.float32)
    values = noise * col_scale[None, :]
    return jnp.clip(values, -8.0, 8.0)


def draw_context(key, part):
    key = jax.random.fold_in(key, 5)
    values = scaled_field(key, TOKENS, HD)
    return values.astype(jnp.bfloat16)


def draw_cotangent(key, part):
    key = jax.random.fold_in(key, 9)
    values = scaled_field(key, TOKENS, D)
    return values.astype(jnp.bfloat16)


def levels(stream_key, dims, pieces, smallest, high):
    gain = 1.0
    for dim, parts in pieces:
        steps = jax.random.uniform(jax.random.fold_in(jax.random.fold_in(stream_key, 6), dim), (parts,), jnp.float32, smallest / len(pieces), high / len(pieces))
        gain = gain * jnp.repeat(jnp.exp(steps), dims[dim] // parts).reshape((-1,) + (1,) * (len(dims) - 1 - dim))
    return gain


def scatter_about(own_key, dims, spread, reach, cuts=(), kind=jnp.bfloat16):
    result = spread * jax.random.normal(own_key, dims, jnp.float32)
    if cuts:
        result = result * levels(own_key, dims, cuts, -0.22, 0.18)
    return jnp.clip(result, -reach, reach).astype(kind)


def setup_inputs(seed: int = 0) -> dict:
    streams_of = jax.random.split(jax.random.key(seed), 6)
    context = draw_context(jax.random.fold_in(streams_of[5], 71), 0)
    cotangent = draw_cotangent(jax.random.fold_in(streams_of[5], 71), 0)
    master_weight = scatter_about(streams_of[2], (HD, D), D ** -0.5, 0.09375, ((0, 512),), jnp.float32)
    row_state = jnp.clip(jnp.exp(math.log(1.0) - 2.3025851 * jax.random.uniform(streams_of[3], (HD,), jnp.float32) ** levels(streams_of[3], (HD,), ((0, 512),), -0.2, 0.2)), 0.1, 1.0)
    col_state = jnp.clip(jnp.exp(jax.random.uniform(streams_of[4], (D,), jnp.float32, math.log(0.16666667), math.log(1.6666666))), 0.16666667, 1.6666666)
    return {"context": context, "cotangent": cotangent, "master_weight": master_weight, "row_state": row_state, "col_state": col_state}


BETA = 0.8
EPS1 = 1e-30
CLIP = 1.0

def reference(context, cotangent, master_weight, row_state, col_state):
    weight_copy = master_weight.astype(jnp.bfloat16)
    grad_input = jnp.dot(cotangent, weight_copy.T, preferred_element_type=jnp.float32).astype(jnp.bfloat16)
    grad = jnp.dot(context.T, cotangent, preferred_element_type=jnp.float32) * (1.0 / TOKENS)
    squared = grad * grad + EPS1
    row_new = BETA * row_state + (1.0 - BETA) * lax.optimization_barrier(jnp.sum(squared, axis=1))
    col_new = BETA * col_state + (1.0 - BETA) * lax.optimization_barrier(jnp.sum(squared, axis=0))
    total = jnp.sum(row_new)
    scaled = grad / jnp.sqrt(row_new[:, None] * col_new[None, :] / total)
    update_rms = jnp.sqrt(jnp.mean(scaled * scaled))
    update = scaled / jnp.maximum(CLIP, update_rms)
    return (grad_input, update, row_new, col_new, update_rms)
```

```python
import jax
import jax.numpy as jnp
from jax import lax
from jax.sharding import Mesh, PartitionSpec as P

BETA = 0.8
EPS1 = 1e-30
CLIP = 1.0
OTHER = ("z", "x", "c")


def spread(value, axes, size):
    copies = jnp.broadcast_to(value[None], (size,) + value.shape)
    return lax.all_to_all(copies, axes, 0, 0, tiled=True)


def on_device(context, cotangent, master_weight, row_state, col_state):
    ny, nz = lax.axis_size("y"), lax.axis_size("z")
    nmp = lax.axis_size("x") * lax.axis_size("c")
    n_other = nz * nmp
    rows, cols = master_weight.shape
    inv_tokens = 1.0 / (cotangent.shape[0] * ny * nz)
    entries = rows * ny * nz * nmp * cols

    term = (
        lax.dot_general(
            context, cotangent, (((0,), (0,)), ((), ())), preferred_element_type=jnp.float32
        )
        * inv_tokens
    )
    part = lax.psum_scatter(term, "y", scatter_dimension=0, tiled=True)

    weight_copy, _ = lax.optimization_barrier((master_weight.astype(jnp.bfloat16), term))
    weight_rows = spread(weight_copy, "z", nz).reshape(nz * rows, cols)
    weight_rows, part = lax.optimization_barrier((weight_rows, part))
    weight = lax.all_gather(weight_rows, "y", axis=0, tiled=True)
    grad_input = lax.dot_general(
        cotangent, weight, (((1,), (1,)), ((), ())), preferred_element_type=jnp.float32
    ).astype(jnp.bfloat16)

    grad = jnp.sum(
        lax.all_to_all(part.reshape(nz, rows, cols), "z", 0, 0, tiled=True), axis=0
    )
    squared = grad * grad + EPS1
    row_new = BETA * row_state + (1.0 - BETA) * jnp.sum(squared, axis=1)
    col_part = jnp.sum(squared, axis=0)
    ratio_part = jnp.sum(grad * grad / row_new[:, None], axis=0)
    lanes = 2 * cols // n_other
    sums = jnp.concatenate([col_part, ratio_part]).reshape(n_other, 1, lanes)
    extra = jnp.broadcast_to(jnp.sum(row_new), (n_other, 1, lanes))
    packed = jnp.concatenate([sums, extra], axis=1)
    packed = jnp.sum(lax.all_to_all(packed, OTHER, 0, 0, tiled=True), axis=0)
    packed = jnp.sum(spread(packed, "y", ny), axis=0)
    packed = spread(packed, OTHER, n_other)
    both = packed[:, 0].reshape(2, cols)
    row_total = packed[0, 1, 0]
    col_new = BETA * col_state + (1.0 - BETA) * both[0]
    update_rms = jnp.sqrt(row_total * jnp.sum(both[1] / col_new) / entries)
    scaled = grad / jnp.sqrt(row_new[:, None] * col_new[None, :] / row_total)
    update = scaled / jnp.maximum(CLIP, update_rms)
    return (grad_input, update, row_new, col_new, update_rms)


def solution(mesh):
    grid = Mesh(mesh.devices.reshape(8, 8, 4, 2), ("y", "z", "x", "c"))
    dp, mp = ("y", "z"), ("x", "c")
    in_specs = (P(dp, mp), P(dp, None), P(mp + dp, None), P(mp + dp), P())
    out_specs = (P(dp, mp), P(mp + dp, None), P(mp + dp), P(), P())
    return jax.shard_map(
        on_device, mesh=grid, in_specs=in_specs, out_specs=out_specs, check_vma=False
    )
```

```python
import jax
import jax.numpy as jnp
from jax import lax
from jax.sharding import Mesh, PartitionSpec as P

BETA = 0.8
EPS1 = 1e-30
CLIP = 1.0
OTHER = ("z", "x", "c")


def spread(value, axes, size):
    copies = jnp.broadcast_to(value[None], (size,) + value.shape)
    return lax.all_to_all(copies, axes, 0, 0, tiled=True)


def on_device(context, cotangent, master_weight, row_state, col_state):
    ny, nz = lax.axis_size("y"), lax.axis_size("z")
    nmp = lax.axis_size("x") * lax.axis_size("c")
    n_other = nz * nmp
    rows, cols = master_weight.shape
    inv_tokens = 1.0 / (cotangent.shape[0] * ny * nz)
    entries = rows * ny * nz * nmp * cols

    term = (
        lax.dot_general(
            context, cotangent, (((0,), (0,)), ((), ())), preferred_element_type=jnp.float32
        )
        * inv_tokens
    )
    part = lax.psum_scatter(term, "y", scatter_dimension=0, tiled=True)

    weight_copy, _ = lax.optimization_barrier((master_weight.astype(jnp.bfloat16), term))
    weight_rows = spread(weight_copy, "z", nz).reshape(nz * rows, cols)
    terms = lax.all_to_all(part.reshape(nz, rows, cols), "z", 0, 0, tiled=True)
    weight_rows, terms = lax.optimization_barrier((weight_rows, terms))
    weight = lax.all_gather(weight_rows, "y", axis=0, tiled=True)
    grad_input = lax.dot_general(
        cotangent, weight, (((1,), (1,)), ((), ())), preferred_element_type=jnp.float32
    ).astype(jnp.bfloat16)

    grad = jnp.sum(terms, axis=0)
    squared = grad * grad + EPS1
    row_new = BETA * row_state + (1.0 - BETA) * jnp.sum(squared, axis=1)
    col_part = jnp.sum(squared, axis=0)
    ratio_part = jnp.sum(grad * grad / row_new[:, None], axis=0)
    lanes = 2 * cols // n_other
    sums = jnp.concatenate([col_part, ratio_part]).reshape(n_other, 1, lanes)
    extra = jnp.broadcast_to(jnp.sum(row_new), (n_other, 1, lanes))
    packed = jnp.concatenate([sums, extra], axis=1)
    packed = jnp.sum(lax.all_to_all(packed, OTHER, 0, 0, tiled=True), axis=0)
    packed = jnp.sum(spread(packed, "y", ny), axis=0)
    packed = spread(packed, OTHER, n_other)
    both = packed[:, 0].reshape(2, cols)
    row_total = packed[0, 1, 0]
    col_new = BETA * col_state + (1.0 - BETA) * both[0]
    update_rms = jnp.sqrt(row_total * jnp.sum(both[1] / col_new) / entries)
    scaled = grad / jnp.sqrt(row_new[:, None] * col_new[None, :] / row_total)
    update = scaled / jnp.maximum(CLIP, update_rms)
    return (grad_input, update, row_new, col_new, update_rms)


def solution(mesh):
    grid = Mesh(mesh.devices.reshape(8, 8, 4, 2), ("y", "z", "x", "c"))
    dp, mp = ("y", "z"), ("x", "c")
    in_specs = (P(dp, mp), P(dp, None), P(mp + dp, None), P(mp + dp), P())
    out_specs = (P(dp, mp), P(mp + dp, None), P(mp + dp), P(), P())
    return jax.shard_map(
        on_device, mesh=grid, in_specs=in_specs, out_specs=out_specs, check_vma=False
    )
```

```python
import jax
import jax.numpy as jnp
from jax import lax
from jax.sharding import Mesh, PartitionSpec as P

BETA = 0.8
EPS1 = 1e-30
CLIP = 1.0
OTHER = ("z", "x", "c")


def spread(value, axes, size):
    copies = jnp.broadcast_to(value[None], (size,) + value.shape)
    return lax.all_to_all(copies, axes, 0, 0, tiled=True)


def on_device(context, cotangent, master_weight, row_state, col_state):
    ny, nz = lax.axis_size("y"), lax.axis_size("z")
    nmp = lax.axis_size("x") * lax.axis_size("c")
    n_other = nz * nmp
    rows, cols = master_weight.shape
    inv_tokens = 1.0 / (cotangent.shape[0] * ny * nz)
    entries = rows * ny * nz * nmp * cols

    weight = lax.all_gather(master_weight.astype(jnp.bfloat16), ("y", "z"), axis=0, tiled=True)
    grad_input = lax.dot_general(
        cotangent, weight, (((1,), (1,)), ((), ())), preferred_element_type=jnp.float32
    ).astype(jnp.bfloat16)

    bound = (
        cotangent.shape[0]
        * jnp.max(jnp.abs(context)).astype(jnp.float32)
        * jnp.max(jnp.abs(cotangent)).astype(jnp.float32)
    )
    power = jnp.clip(jnp.floor(jnp.log2(bound)), -100.0, 14.0)
    term = lax.dot_general(
        context, cotangent, (((0,), (0,)), ((), ())), preferred_element_type=jnp.float32
    )
    coded = (term * jnp.exp2(14.0 - power)).astype(jnp.float16).reshape(ny * nz, rows, cols)
    coded = jnp.concatenate(
        [coded, jnp.broadcast_to(power.astype(jnp.float16), (ny * nz, rows, 128))], axis=2
    )
    coded = lax.all_to_all(coded, ("y", "z"), 0, 0, tiled=True)
    scales = jnp.exp2(coded[:, :1, cols:cols + 1].astype(jnp.float32) - 14.0)
    grad = jnp.sum(coded[:, :, :cols].astype(jnp.float32) * scales, axis=0) * inv_tokens
    squared = grad * grad + EPS1
    row_new = BETA * row_state + (1.0 - BETA) * jnp.sum(squared, axis=1)
    col_part = jnp.sum(squared, axis=0)
    ratio_part = jnp.sum(grad * grad / row_new[:, None], axis=0)
    lanes = 2 * cols // n_other
    sums = jnp.concatenate([col_part, ratio_part]).reshape(n_other, 1, lanes)
    extra = jnp.broadcast_to(jnp.sum(row_new), (n_other, 1, lanes))
    packed = jnp.concatenate([sums, extra], axis=1)
    packed = jnp.sum(lax.all_to_all(packed, OTHER, 0, 0, tiled=True), axis=0)
    packed = jnp.sum(spread(packed, "y", ny), axis=0)
    packed = spread(packed, OTHER, n_other)
    both = packed[:, 0].reshape(2, cols)
    row_total = packed[0, 1, 0]
    col_new = BETA * col_state + (1.0 - BETA) * both[0]
    update_rms = jnp.sqrt(row_total * jnp.sum(both[1] / col_new) / entries)
    scaled = grad / jnp.sqrt(row_new[:, None] * col_new[None, :] / row_total)
    update = scaled / jnp.maximum(CLIP, update_rms)
    return (grad_input, update, row_new, col_new, update_rms)


def solution(mesh):
    grid = Mesh(mesh.devices.reshape(8, 8, 4, 2), ("y", "z", "x", "c"))
    dp, mp = ("y", "z"), ("x", "c")
    in_specs = (P(dp, mp), P(dp, None), P(mp + dp, None), P(mp + dp), P())
    out_specs = (P(dp, mp), P(mp + dp, None), P(mp + dp), P(), P())
    return jax.shard_map(
        on_device, mesh=grid, in_specs=in_specs, out_specs=out_specs, check_vma=False
    )
```

```python
import functools

import jax
import jax.numpy as jnp
from jax import lax
from jax.experimental import pallas as pl
from jax.experimental.pallas import tpu as pltpu
from jax.sharding import Mesh, PartitionSpec as P

BETA = 0.8
EPS1 = 1e-30
CLIP = 1.0
CHUNK = 512
LANES = 128
OTHER = ("z", "x", "c")
VMEM = pl.BlockSpec(memory_space=pltpu.VMEM)
PARAMS = pltpu.CompilerParams(vmem_limit_bytes=32 * 2**20)


def term_kernel(inv_tokens, context_ref, left_ref, right_ref, out_ref):
    peers, rows = out_ref.shape[0], out_ref.shape[1] // 2
    for half, cotangent_ref in enumerate((left_ref, right_ref)):
        term = lax.dot_general(
            context_ref[...],
            cotangent_ref[...],
            (((0,), (0,)), ((), ())),
            preferred_element_type=jnp.float32,
        )
        out_ref[:, half * rows:(half + 1) * rows, :] = (term * inv_tokens).reshape(
            peers, rows, term.shape[1]
        )


def term_of(context, cotangent, inv_tokens, peers, rows):
    tokens, cols = cotangent.shape
    steps = cols // (2 * CHUNK)
    return pl.pallas_call(
        functools.partial(term_kernel, inv_tokens),
        grid=(steps,),
        out_shape=jax.ShapeDtypeStruct((peers, 2 * rows, cols // 2), jnp.float32),
        in_specs=[
            pl.BlockSpec((tokens, context.shape[1]), lambda i: (0, 0)),
            pl.BlockSpec((tokens, CHUNK), lambda i: (0, i)),
            pl.BlockSpec((tokens, CHUNK), lambda i: (0, i + steps)),
        ],
        out_specs=pl.BlockSpec((peers, 2 * rows, CHUNK), lambda i: (0, 0, i)),
        compiler_params=pltpu.CompilerParams(vmem_limit_bytes=60 * 2**20),
        cost_estimate=pl.CostEstimate(
            flops=2 * tokens * context.shape[1] * cols,
            bytes_accessed=2 * tokens * cols + 4 * peers * rows * cols,
            transcendentals=0,
        ),
        name="term",
    )(context, cotangent, cotangent)


def sums_kernel(pieces_ref, state_ref, grad_ref, row_ref, packed_ref):
    grad = pieces_ref[0]
    for k in range(1, pieces_ref.shape[0]):
        grad = grad + pieces_ref[k]
    grad_ref[...] = grad
    rows = grad.shape[0] // 2
    plain = grad * grad
    squared = plain + EPS1
    row_sum = jnp.sum(squared, axis=1, keepdims=True)
    row_new = BETA * state_ref[...] + (1.0 - BETA) * (row_sum[:rows] + row_sum[rows:])
    row_ref[...] = row_new
    ratio = plain * (1.0 / jnp.concatenate([row_new, row_new], axis=0))
    per_half = grad.shape[1] // LANES
    packed_ref[:, 1:, :] = jnp.broadcast_to(
        jnp.sum(row_new, axis=0, keepdims=True).reshape(1, 1, 1), (packed_ref.shape[0], 1, LANES)
    )
    for which, value in enumerate((squared, ratio)):
        for half in range(2):
            total = jnp.sum(value[half * rows:(half + 1) * rows], axis=0, keepdims=True)
            for i in range(per_half):
                place = (2 * which + half) * per_half + i
                packed_ref[place, :1, :] = total[:, i * LANES:(i + 1) * LANES]


def sums_of(pieces, row_state, peers):
    count, rows, cols = pieces.shape
    return pl.pallas_call(
        sums_kernel,
        out_shape=(
            jax.ShapeDtypeStruct((rows, cols), jnp.float32),
            jax.ShapeDtypeStruct(row_state.shape, jnp.float32),
            jax.ShapeDtypeStruct((peers, 2, LANES), jnp.float32),
        ),
        in_specs=[VMEM] * 2,
        out_specs=(VMEM,) * 3,
        compiler_params=PARAMS,
        name="sums",
    )(pieces, row_state)


def update_kernel(entries, sums_ref, total_ref, grad_ref, row_ref, state_ref, out_ref, col_ref, rms_ref):
    groups = col_ref.shape[0]
    total = total_ref[:1, :1]
    col_new = BETA * state_ref[...] + (1.0 - BETA) * sums_ref[:groups]
    col_ref[...] = col_new
    ratio = sums_ref[groups:] / col_new
    ratio = jnp.sum(jnp.sum(ratio, axis=0, keepdims=True), axis=1, keepdims=True)
    rms = jnp.sqrt(total * ratio / entries)
    rms_ref[...] = rms
    clip = jnp.maximum(CLIP, rms)
    rows = row_ref.shape[0]
    row = row_ref[...]
    for i in range(groups):
        half, start = divmod(i, groups // 2)
        start *= LANES
        grad = grad_ref[half * rows:(half + 1) * rows, start:start + LANES]
        scaled = grad / jnp.sqrt(row * col_new[i:i + 1] / total)
        out_ref[:, i * LANES:(i + 1) * LANES] = scaled / clip


def update_of(sums, total, grad, row_new, state, entries):
    rows, cols = row_new.shape[0], 2 * grad.shape[1]
    return pl.pallas_call(
        functools.partial(update_kernel, entries),
        out_shape=(
            jax.ShapeDtypeStruct((rows, cols), jnp.float32),
            jax.ShapeDtypeStruct(state.shape, jnp.float32),
            jax.ShapeDtypeStruct((1, 1), jnp.float32),
        ),
        in_specs=[VMEM] * 5,
        out_specs=(VMEM,) * 3,
        compiler_params=PARAMS,
        name="update",
    )(sums, total, grad, row_new, state)


def spread(value, axes, size):
    copies = jnp.broadcast_to(value[None], (size,) + value.shape)
    return lax.all_to_all(copies, axes, 0, 0, tiled=True)


def on_device(context, cotangent, master_weight, row_state, col_state):
    ny, nz = lax.axis_size("y"), lax.axis_size("z")
    nmp = lax.axis_size("x") * lax.axis_size("c")
    n_other = nz * nmp
    rows, cols = master_weight.shape
    inv_tokens = 1.0 / (cotangent.shape[0] * ny * nz)
    entries = rows * ny * nz * nmp * cols

    term = term_of(context, cotangent, inv_tokens, ny * nz, rows)
    part = lax.psum_scatter(
        term.reshape(ny * nz * 2 * rows, cols // 2), "y", scatter_dimension=0, tiled=True
    )

    weight_copy, _ = lax.optimization_barrier((master_weight.astype(jnp.bfloat16), term))
    weight_rows = spread(weight_copy, "z", nz).reshape(nz * rows, cols)
    weight_rows, part = lax.optimization_barrier((weight_rows, part))
    weight = lax.all_gather(weight_rows, "y", axis=0, tiled=True)
    grad_input = lax.dot_general(
        cotangent, weight, (((1,), (1,)), ((), ())), preferred_element_type=jnp.float32
    ).astype(jnp.bfloat16)

    pieces = lax.all_to_all(part.reshape(nz, 2 * rows, cols // 2), "z", 0, 0, tiled=True)
    grad, row_new, packed = sums_of(pieces, row_state[:, None], n_other)
    packed = jnp.sum(lax.all_to_all(packed, OTHER, 0, 0, tiled=True), axis=0)
    packed = jnp.sum(spread(packed, "y", ny), axis=0)
    packed = spread(packed, OTHER, n_other)
    packed, grad_input = lax.optimization_barrier((packed, grad_input))
    update, col_new, update_rms = update_of(
        packed[:, 0], packed[0, 1:], grad, row_new, col_state.reshape(cols // LANES, LANES), entries
    )
    return (grad_input, update, row_new[:, 0], col_new.reshape(cols), update_rms[0, 0])


def solution(mesh):
    grid = Mesh(mesh.devices.reshape(8, 8, 4, 2), ("y", "z", "x", "c"))
    dp, mp = ("y", "z"), ("x", "c")
    in_specs = (P(dp, mp), P(dp, None), P(mp + dp, None), P(mp + dp), P())
    out_specs = (P(dp, mp), P(mp + dp, None), P(mp + dp), P(), P())
    return jax.shard_map(
        on_device, mesh=grid, in_specs=in_specs, out_specs=out_specs, check_vma=False
    )
```

```python
import functools

import jax
import jax.numpy as jnp
from jax import lax
from jax.experimental import pallas as pl
from jax.experimental.pallas import tpu as pltpu
from jax.sharding import Mesh, PartitionSpec as P

BETA = 0.8
EPS1 = 1e-30
CLIP = 1.0
CHUNK = 512
LANES = 128
NEAR = ("x", "c")
FAR = ("y", "z")
VMEM = pl.BlockSpec(memory_space=pltpu.VMEM)
PARAMS = pltpu.CompilerParams(vmem_limit_bytes=32 * 2**20)


def term_kernel(inv_tokens, context_ref, left_ref, right_ref, out_ref):
    peers, rows = out_ref.shape[0], out_ref.shape[1] // 2
    for half, cotangent_ref in enumerate((left_ref, right_ref)):
        term = lax.dot_general(
            context_ref[...],
            cotangent_ref[...],
            (((0,), (0,)), ((), ())),
            preferred_element_type=jnp.float32,
        )
        out_ref[:, half * rows:(half + 1) * rows, :] = (term * inv_tokens).reshape(
            peers, rows, term.shape[1]
        )


def term_of(context, cotangent, inv_tokens, peers, rows):
    tokens, cols = cotangent.shape
    steps = cols // (2 * CHUNK)
    return pl.pallas_call(
        functools.partial(term_kernel, inv_tokens),
        grid=(steps,),
        out_shape=jax.ShapeDtypeStruct((peers, 2 * rows, cols // 2), jnp.float32),
        in_specs=[
            pl.BlockSpec((tokens, context.shape[1]), lambda i: (0, 0)),
            pl.BlockSpec((tokens, CHUNK), lambda i: (0, i)),
            pl.BlockSpec((tokens, CHUNK), lambda i: (0, i + steps)),
        ],
        out_specs=pl.BlockSpec((peers, 2 * rows, CHUNK), lambda i: (0, 0, i)),
        compiler_params=pltpu.CompilerParams(vmem_limit_bytes=60 * 2**20),
        cost_estimate=pl.CostEstimate(
            flops=2 * tokens * context.shape[1] * cols,
            bytes_accessed=2 * tokens * cols + 4 * peers * rows * cols,
            transcendentals=0,
        ),
        name="term",
    )(context, cotangent, cotangent)


def sums_kernel(pieces_ref, state_ref, grad_ref, row_ref, packed_ref):
    grad = pieces_ref[0]
    for k in range(1, pieces_ref.shape[0]):
        grad = grad + pieces_ref[k]
    grad_ref[...] = grad
    rows = grad.shape[0] // 2
    plain = grad * grad
    squared = plain + EPS1
    row_sum = jnp.sum(squared, axis=1, keepdims=True)
    row_new = BETA * state_ref[...] + (1.0 - BETA) * (row_sum[:rows] + row_sum[rows:])
    row_ref[...] = row_new
    ratio = plain * (1.0 / jnp.concatenate([row_new, row_new], axis=0))
    per_half = grad.shape[1] // LANES
    for which, value in enumerate((squared, ratio)):
        for half in range(2):
            total = jnp.sum(value[half * rows:(half + 1) * rows], axis=0, keepdims=True)
            for i in range(per_half):
                place = (2 * which + half) * per_half + i
                group, line = divmod(place, packed_ref.shape[1])
                packed_ref[group, line:line + 1, :] = total[:, i * LANES:(i + 1) * LANES]


def sums_of(pieces, row_state, peers):
    count, rows, cols = pieces.shape
    return pl.pallas_call(
        sums_kernel,
        out_shape=(
            jax.ShapeDtypeStruct((rows, cols), jnp.float32),
            jax.ShapeDtypeStruct(row_state.shape, jnp.float32),
            jax.ShapeDtypeStruct((peers, 2 * 2 * cols // (peers * LANES), LANES), jnp.float32),
        ),
        in_specs=[VMEM] * 2,
        out_specs=(VMEM,) * 3,
        compiler_params=PARAMS,
        name="sums",
    )(pieces, row_state)


def update_kernel(entries, sums_ref, total_ref, grad_ref, row_ref, state_ref, out_ref, col_ref, rms_ref):
    groups = col_ref.shape[0]
    total = jnp.sum(jnp.sum(sums_ref[:groups], axis=0, keepdims=True), axis=1, keepdims=True)
    total = BETA * total_ref[:1, :1] + (1.0 - BETA) * total
    col_new = BETA * state_ref[...] + (1.0 - BETA) * sums_ref[:groups]
    col_ref[...] = col_new
    ratio = sums_ref[groups:] / col_new
    ratio = jnp.sum(jnp.sum(ratio, axis=0, keepdims=True), axis=1, keepdims=True)
    rms = jnp.sqrt(total * ratio / entries)
    rms_ref[...] = rms
    clip = jnp.maximum(CLIP, rms)
    rows = row_ref.shape[0]
    row = row_ref[...]
    for i in range(groups):
        half, start = divmod(i, groups // 2)
        start *= LANES
        grad = grad_ref[half * rows:(half + 1) * rows, start:start + LANES]
        scaled = grad / jnp.sqrt(row * col_new[i:i + 1] / total)
        out_ref[:, i * LANES:(i + 1) * LANES] = scaled / clip


def update_of(sums, total, grad, row_new, state, entries):
    rows, cols = row_new.shape[0], 2 * grad.shape[1]
    return pl.pallas_call(
        functools.partial(update_kernel, entries),
        out_shape=(
            jax.ShapeDtypeStruct((rows, cols), jnp.float32),
            jax.ShapeDtypeStruct(state.shape, jnp.float32),
            jax.ShapeDtypeStruct((1, 1), jnp.float32),
        ),
        in_specs=[VMEM] * 5,
        out_specs=(VMEM,) * 3,
        compiler_params=PARAMS,
        name="update",
    )(sums, total, grad, row_new, state)


def fold_kernel(value_ref, out_ref):
    total = jnp.sum(value_ref[...], axis=0, keepdims=True)
    out_ref[...] = jnp.broadcast_to(total, out_ref.shape)


def fold(value, copies):
    return pl.pallas_call(
        fold_kernel,
        out_shape=jax.ShapeDtypeStruct((copies,) + value.shape[1:], value.dtype),
        in_specs=[VMEM],
        out_specs=VMEM,
        compiler_params=PARAMS,
        name="fold",
    )(value)


def exchange(value, axes):
    return lax.all_to_all(value, axes, 0, 0, tiled=True)


def on_device(context, cotangent, master_weight, row_state, col_state):
    ny, nz = lax.axis_size("y"), lax.axis_size("z")
    nmp = lax.axis_size("x") * lax.axis_size("c")
    rows, cols = master_weight.shape
    inv_tokens = 1.0 / (cotangent.shape[0] * ny * nz)
    entries = rows * ny * nz * nmp * cols

    term = term_of(context, cotangent, inv_tokens, ny * nz, rows)
    part = lax.psum_scatter(
        term.reshape(ny * nz * 2 * rows, cols // 2), "y", scatter_dimension=0, tiled=True
    )

    weight_copy, row_state, _ = lax.optimization_barrier(
        (master_weight.astype(jnp.bfloat16), row_state, term)
    )
    copies = jnp.broadcast_to(weight_copy[None], (nz, rows, cols))
    weight_rows = exchange(copies, "z").reshape(nz * rows, cols)
    state_sum = jnp.broadcast_to(jnp.sum(row_state), (nmp, 1, LANES))
    state_sum = fold(exchange(fold(exchange(state_sum, NEAR), ny * nz), FAR), 1)[0]
    weight_rows, part, state_sum = lax.optimization_barrier((weight_rows, part, state_sum))
    weight = lax.all_gather(weight_rows, "y", axis=0, tiled=True)
    grad_input = lax.dot_general(
        cotangent, weight, (((1,), (1,)), ((), ())), preferred_element_type=jnp.float32
    ).astype(jnp.bfloat16)

    pieces = exchange(part.reshape(nz, 2 * rows, cols // 2), "z")
    grad, row_new, packed = sums_of(pieces, row_state[:, None], nmp)
    packed = fold(exchange(packed, NEAR), ny * nz)
    packed = fold(exchange(packed, FAR), nmp)
    packed = exchange(packed, NEAR).reshape(2 * cols // LANES, LANES)
    packed, grad_input = lax.optimization_barrier((packed, grad_input))
    update, col_new, update_rms = update_of(
        packed, state_sum, grad, row_new, col_state.reshape(cols // LANES, LANES), entries
    )
    return (grad_input, update, row_new[:, 0], col_new.reshape(cols), update_rms[0, 0])


def solution(mesh):
    grid = Mesh(mesh.devices.reshape(8, 8, 4, 2), ("y", "z", "x", "c"))
    dp, mp = ("y", "z"), ("x", "c")
    in_specs = (P(dp, mp), P(dp, None), P(mp + dp, None), P(mp + dp), P())
    out_specs = (P(dp, mp), P(mp + dp, None), P(mp + dp), P(), P())
    return jax.shard_map(
        on_device, mesh=grid, in_specs=in_specs, out_specs=out_specs, check_vma=False
    )
```

```python
import functools

import jax
import jax.numpy as jnp
from jax import lax
from jax.experimental import pallas as pl
from jax.experimental.pallas import tpu as pltpu
from jax.sharding import Mesh, PartitionSpec as P

BETA = 0.8
EPS1 = 1e-30
CLIP = 1.0
CHUNK = 512
ASIDE = 384
LANES = 128
NEAR = ("x", "c")
FAR = ("y", "z")
VMEM = pl.BlockSpec(memory_space=pltpu.VMEM)
PARAMS = pltpu.CompilerParams(vmem_limit_bytes=32 * 2**20)


def spans(start, stop):
    return [(i, min(CHUNK, stop - i)) for i in range(start, stop, CHUNK)]


def product(context_ref, cotangent, inv_tokens):
    return inv_tokens * lax.dot_general(
        context_ref[...], cotangent, (((0,), (0,)), ((), ())), preferred_element_type=jnp.float32
    )


def term_kernel(inv_tokens, context_hbm, cotangent_hbm, state_ref, out_hbm, context_ref, cotangent_ref, out_ref, in_sems, out_sems):
    peers, rows, width = out_ref.shape[0], out_ref.shape[1] // 2, out_ref.shape[2] - LANES
    half_cols = cotangent_hbm.shape[1] // 2
    first = pltpu.make_async_copy(context_hbm, context_ref, in_sems.at[0])
    first.start()
    loads = []
    for k, (start, size) in enumerate(spans(0, width)):
        for half in range(2):
            place = pl.ds(half * half_cols + start, size)
            copy = pltpu.make_async_copy(
                cotangent_hbm.at[:, place], cotangent_ref.at[:, place], in_sems.at[1 + 2 * k + half]
            )
            copy.start()
            loads.append(copy)
    first.wait()
    stores = []
    for k, (start, size) in enumerate(spans(0, width)):
        for half in range(2):
            loads[2 * k + half].wait()
            place = half * half_cols + start
            term = product(context_ref, cotangent_ref[:, place:place + size], inv_tokens)
            out_ref[:, half * rows:(half + 1) * rows, start:start + size] = term.reshape(
                peers, rows, size
            )
        if start + size == width:
            total = jnp.sum(state_ref[...], axis=1, keepdims=True).reshape(1, 1, 1)
            out_ref[:, :, width:] = jnp.broadcast_to(total, (peers, 2 * rows, LANES))
            size += LANES
        place = pl.ds(start, size)
        copy = pltpu.make_async_copy(
            out_ref.at[:, :, place], out_hbm.at[:, :, place], out_sems.at[k]
        )
        copy.start()
        stores.append(copy)
    for copy in stores:
        copy.wait()


def term_of(context, cotangent, row_state, inv_tokens, peers, rows):
    tokens, cols = cotangent.shape
    width = cols // 2 - ASIDE + LANES
    count = len(spans(0, width - LANES))
    return pl.pallas_call(
        functools.partial(term_kernel, inv_tokens),
        out_shape=jax.ShapeDtypeStruct((peers, 2 * rows, width), jnp.float32),
        in_specs=[pl.BlockSpec(memory_space=pl.ANY)] * 2 + [VMEM],
        out_specs=pl.BlockSpec(memory_space=pl.ANY),
        scratch_shapes=[
            pltpu.VMEM(context.shape, context.dtype),
            pltpu.VMEM(cotangent.shape, cotangent.dtype),
            pltpu.VMEM((peers, 2 * rows, width), jnp.float32),
            pltpu.SemaphoreType.DMA((1 + 2 * count,)),
            pltpu.SemaphoreType.DMA((count,)),
        ],
        compiler_params=pltpu.CompilerParams(vmem_limit_bytes=60 * 2**20),
        cost_estimate=pl.CostEstimate(
            flops=2 * tokens * context.shape[1] * cols,
            bytes_accessed=2 * tokens * cols + 4 * peers * rows * cols,
            transcendentals=0,
        ),
        name="term",
    )(context, cotangent, row_state[None])


def aside_kernel(inv_tokens, context_ref, left_ref, right_ref, out_ref):
    nz, ny, rows, width = out_ref.shape
    rows //= 2
    for half, cotangent_ref in enumerate((left_ref, right_ref)):
        term = product(context_ref, cotangent_ref[...], inv_tokens)
        for y in range(ny):
            part = term[y * nz * rows:(y + 1) * nz * rows]
            out_ref[:, y, half * rows:(half + 1) * rows, :] = part.reshape(nz, rows, width)


def aside_of(context, cotangent, inv_tokens, ny, nz, rows):
    half_cols = cotangent.shape[1] // 2
    left = cotangent[:, half_cols - ASIDE:half_cols]
    right = cotangent[:, 2 * half_cols - ASIDE:]
    return pl.pallas_call(
        functools.partial(aside_kernel, inv_tokens),
        out_shape=jax.ShapeDtypeStruct((nz, ny, 2 * rows, ASIDE), jnp.float32),
        in_specs=[VMEM] * 3,
        out_specs=VMEM,
        compiler_params=PARAMS,
        name="aside",
    )(context, left, right)


def sums_kernel(pieces_ref, aside_ref, state_ref, grad_ref, row_ref, packed_ref):
    most = jnp.sum(pieces_ref[...], axis=0)
    width = most.shape[1] - LANES
    grad = jnp.concatenate([most[:, :width], jnp.sum(aside_ref[...], axis=0)], axis=1)
    grad_ref[...] = grad
    lines = packed_ref.shape[1] // 2
    packed_ref[:, lines:, :] = jnp.broadcast_to(most[None, :lines, width:], (packed_ref.shape[0], lines, LANES))
    rows = grad.shape[0] // 2
    plain = grad * grad
    squared = plain + EPS1
    row_sum = jnp.sum(squared, axis=1, keepdims=True)
    row_new = BETA * state_ref[...] + (1.0 - BETA) * (row_sum[:rows] + row_sum[rows:])
    row_ref[...] = row_new
    ratio = plain * (1.0 / jnp.concatenate([row_new, row_new], axis=0))
    per_half = grad.shape[1] // LANES
    for which, value in enumerate((squared, ratio)):
        for half in range(2):
            total = jnp.sum(value[half * rows:(half + 1) * rows], axis=0, keepdims=True)
            for i in range(per_half):
                place = (2 * which + half) * per_half + i
                group, line = divmod(place, lines)
                packed_ref[group, line:line + 1, :] = total[:, i * LANES:(i + 1) * LANES]


def sums_of(pieces, aside, row_state, peers):
    rows, cols = pieces.shape[1], pieces.shape[2] - LANES + ASIDE
    return pl.pallas_call(
        sums_kernel,
        out_shape=(
            jax.ShapeDtypeStruct((rows, cols), jnp.float32),
            jax.ShapeDtypeStruct(row_state.shape, jnp.float32),
            jax.ShapeDtypeStruct((peers, 2 * 4 * cols // (peers * LANES), LANES), jnp.float32),
        ),
        in_specs=[VMEM] * 3,
        out_specs=(VMEM,) * 3,
        compiler_params=PARAMS,
        name="sums",
    )(pieces, aside, row_state)


def update_kernel(entries, sums_ref, total_ref, grad_ref, row_ref, state_ref, out_ref, col_ref, rms_ref):
    groups = col_ref.shape[0]
    total = jnp.sum(jnp.sum(sums_ref[:groups], axis=0, keepdims=True), axis=1, keepdims=True)
    total = BETA * total_ref[:1, :1] + (1.0 - BETA) * total
    col_new = BETA * state_ref[...] + (1.0 - BETA) * sums_ref[:groups]
    col_ref[...] = col_new
    ratio = sums_ref[groups:] / col_new
    ratio = jnp.sum(jnp.sum(ratio, axis=0, keepdims=True), axis=1, keepdims=True)
    rms = jnp.sqrt(total * ratio / entries)
    rms_ref[...] = rms
    clip = jnp.maximum(CLIP, rms)
    rows = row_ref.shape[0]
    row = row_ref[...]
    for i in range(groups):
        half, start = divmod(i, groups // 2)
        start *= LANES
        grad = grad_ref[half * rows:(half + 1) * rows, start:start + LANES]
        scaled = grad / jnp.sqrt(row * col_new[i:i + 1] / total)
        out_ref[:, i * LANES:(i + 1) * LANES] = scaled / clip


def update_of(sums, total, grad, row_new, state, entries):
    rows, cols = row_new.shape[0], 2 * grad.shape[1]
    return pl.pallas_call(
        functools.partial(update_kernel, entries),
        out_shape=(
            jax.ShapeDtypeStruct((rows, cols), jnp.float32),
            jax.ShapeDtypeStruct(state.shape, jnp.float32),
            jax.ShapeDtypeStruct((1, 1), jnp.float32),
        ),
        in_specs=[VMEM] * 5,
        out_specs=(VMEM,) * 3,
        compiler_params=PARAMS,
        name="update",
    )(sums, total, grad, row_new, state)


def fold_kernel(value_ref, out_ref):
    total = jnp.sum(value_ref[...], axis=0, keepdims=True)
    out_ref[...] = jnp.broadcast_to(total, out_ref.shape)


def fold(value, copies):
    return pl.pallas_call(
        fold_kernel,
        out_shape=jax.ShapeDtypeStruct((copies,) + value.shape[1:], value.dtype),
        in_specs=[VMEM],
        out_specs=VMEM,
        compiler_params=PARAMS,
        name="fold",
    )(value)


def split_kernel(value_ref, out_ref, rest_ref):
    total = jnp.sum(value_ref[...], axis=0, keepdims=True)
    lines = out_ref.shape[1]
    out_ref[...] = jnp.broadcast_to(total[:, :lines], out_ref.shape)
    rest_ref[...] = total[0, lines:]


def split_fold(value, copies):
    lines = value.shape[1] // 2
    return pl.pallas_call(
        split_kernel,
        out_shape=(
            jax.ShapeDtypeStruct((copies, lines, LANES), value.dtype),
            jax.ShapeDtypeStruct((lines, LANES), value.dtype),
        ),
        in_specs=[VMEM],
        out_specs=(VMEM,) * 2,
        compiler_params=PARAMS,
        name="split_fold",
    )(value)


def exchange(value, axes):
    return lax.all_to_all(value, axes, 0, 0, tiled=True)


def on_device(context, cotangent, master_weight, row_state, col_state):
    ny, nz = lax.axis_size("y"), lax.axis_size("z")
    nmp = lax.axis_size("x") * lax.axis_size("c")
    rows, cols = master_weight.shape
    inv_tokens = 1.0 / (cotangent.shape[0] * ny * nz)
    entries = rows * ny * nz * nmp * cols

    term = term_of(context, cotangent, row_state, inv_tokens, ny * nz, rows)
    part = lax.psum_scatter(
        term.reshape(ny * nz * 2 * rows, term.shape[2]), "y", scatter_dimension=0, tiled=True
    )
    weight_copy, context, _ = lax.optimization_barrier(
        (master_weight.astype(jnp.bfloat16), context, term)
    )
    copies = jnp.broadcast_to(weight_copy[None], (nz, rows, cols))
    weight_rows = exchange(copies, "z").reshape(nz * rows, cols)
    aside = exchange(aside_of(context, cotangent, inv_tokens, ny, nz, rows), "z")
    aside = exchange(jnp.sum(aside, axis=0), "y")
    weight_rows, part, aside = lax.optimization_barrier((weight_rows, part, aside))
    weight = lax.all_gather(weight_rows, "y", axis=0, tiled=True)
    grad_input = lax.dot_general(
        cotangent, weight, (((1,), (1,)), ((), ())), preferred_element_type=jnp.float32
    ).astype(jnp.bfloat16)

    pieces = exchange(part.reshape(nz, 2 * rows, term.shape[2]), "z")
    grad, row_new, packed = sums_of(pieces, aside, row_state[:, None], nmp)
    packed, state_sum = split_fold(exchange(packed, NEAR), ny * nz)
    packed = fold(exchange(packed, FAR), nmp)
    packed = exchange(packed, NEAR).reshape(2 * cols // LANES, LANES)
    packed, grad_input = lax.optimization_barrier((packed, grad_input))
    update, col_new, update_rms = update_of(
        packed, state_sum, grad, row_new, col_state.reshape(cols // LANES, LANES), entries
    )
    return (grad_input, update, row_new[:, 0], col_new.reshape(cols), update_rms[0, 0])


def solution(mesh):
    grid = Mesh(mesh.devices.reshape(8, 8, 4, 2), ("y", "z", "x", "c"))
    dp, mp = ("y", "z"), ("x", "c")
    in_specs = (P(dp, mp), P(dp, None), P(mp + dp, None), P(mp + dp), P())
    out_specs = (P(dp, mp), P(mp + dp, None), P(mp + dp), P(), P())
    return jax.shard_map(
        on_device, mesh=grid, in_specs=in_specs, out_specs=out_specs, check_vma=False
    )
```

```python
import functools

import jax
import jax.numpy as jnp
from jax import lax
from jax.experimental import pallas as pl
from jax.experimental.pallas import tpu as pltpu
from jax.sharding import Mesh, PartitionSpec as P

BETA = 0.8
EPS1 = 1e-30
CLIP = 1.0
CHUNK = 512
ASIDE = 512
LANES = 128
NEAR = ("x", "c")
FAR = ("y", "z")
VMEM = pl.BlockSpec(memory_space=pltpu.VMEM)
PARAMS = pltpu.CompilerParams(vmem_limit_bytes=32 * 2**20)


def spans(start, stop):
    return [(i, min(CHUNK, stop - i)) for i in range(start, stop, CHUNK)]


def product(context_ref, cotangent, inv_tokens):
    return inv_tokens * lax.dot_general(
        context_ref[...], cotangent, (((0,), (0,)), ((), ())), preferred_element_type=jnp.float32
    )


def term_kernel(inv_tokens, context_hbm, cotangent_hbm, state_ref, out_hbm, context_ref, cotangent_ref, out_ref, in_sems, out_sems):
    peers, rows, width = out_ref.shape[0], out_ref.shape[1] // 2, out_ref.shape[2] - LANES
    half_cols = cotangent_hbm.shape[1] // 2
    first = pltpu.make_async_copy(context_hbm, context_ref, in_sems.at[0])
    first.start()
    loads = []
    for k, (start, size) in enumerate(spans(0, width)):
        for half in range(2):
            place = pl.ds(half * half_cols + start, size)
            copy = pltpu.make_async_copy(
                cotangent_hbm.at[:, place], cotangent_ref.at[:, place], in_sems.at[1 + 2 * k + half]
            )
            copy.start()
            loads.append(copy)
    first.wait()
    stores = []
    for k, (start, size) in enumerate(spans(0, width)):
        for half in range(2):
            loads[2 * k + half].wait()
            place = half * half_cols + start
            term = product(context_ref, cotangent_ref[:, place:place + size], inv_tokens)
            out_ref[:, half * rows:(half + 1) * rows, start:start + size] = term.reshape(
                peers, rows, size
            )
        if start + size == width:
            total = jnp.sum(state_ref[...], axis=1, keepdims=True).reshape(1, 1, 1)
            out_ref[:, :, width:] = jnp.broadcast_to(total, (peers, 2 * rows, LANES))
            size += LANES
        place = pl.ds(start, size)
        copy = pltpu.make_async_copy(
            out_ref.at[:, :, place], out_hbm.at[:, :, place], out_sems.at[k]
        )
        copy.start()
        stores.append(copy)
    for copy in stores:
        copy.wait()


def term_of(context, cotangent, row_state, inv_tokens, peers, rows):
    tokens, cols = cotangent.shape
    width = cols // 2 - ASIDE + LANES
    count = len(spans(0, width - LANES))
    return pl.pallas_call(
        functools.partial(term_kernel, inv_tokens),
        out_shape=jax.ShapeDtypeStruct((peers, 2 * rows, width), jnp.float32),
        in_specs=[pl.BlockSpec(memory_space=pl.ANY)] * 2 + [VMEM],
        out_specs=pl.BlockSpec(memory_space=pl.ANY),
        scratch_shapes=[
            pltpu.VMEM(context.shape, context.dtype),
            pltpu.VMEM(cotangent.shape, cotangent.dtype),
            pltpu.VMEM((peers, 2 * rows, width), jnp.float32),
            pltpu.SemaphoreType.DMA((1 + 2 * count,)),
            pltpu.SemaphoreType.DMA((count,)),
        ],
        compiler_params=pltpu.CompilerParams(vmem_limit_bytes=60 * 2**20),
        cost_estimate=pl.CostEstimate(
            flops=2 * tokens * context.shape[1] * cols,
            bytes_accessed=2 * tokens * cols + 4 * peers * rows * cols,
            transcendentals=0,
        ),
        name="term",
    )(context, cotangent, row_state[None])


def aside_kernel(inv_tokens, context_ref, left_ref, right_ref, weight_ref, out_ref, term_ref):
    nz, ny, rows, _ = term_ref.shape
    rows //= 2
    for half, cotangent_ref in enumerate((left_ref, right_ref)):
        term = product(context_ref, cotangent_ref[...], inv_tokens)
        for y in range(ny):
            part = term[y * nz * rows:(y + 1) * nz * rows]
            term_ref[:, y, half * rows:(half + 1) * rows, :] = part.reshape(nz, rows, ASIDE)
    for z in range(nz):
        term = term_ref[z]
        upper = term.astype(jnp.bfloat16).astype(jnp.float32)
        both = jnp.concatenate([upper, term - upper], axis=1)
        out_ref[z, :, :, :ASIDE] = both.astype(jnp.bfloat16)
    size = out_ref.shape[3] - ASIDE
    groups = out_ref.shape[2] // rows
    for y in range(ny):
        starts = [(y * groups + q) * size for q in range(groups)]
        part = jnp.concatenate([weight_ref[:, i:i + size] for i in starts], axis=0)
        out_ref[:, y, :, ASIDE:] = jnp.broadcast_to(part[None], (nz,) + part.shape).astype(
            jnp.bfloat16
        )


def aside_of(context, cotangent, weight, inv_tokens, ny, nz):
    rows, cols = weight.shape
    left = cotangent[:, cols // 2 - ASIDE:cols // 2]
    right = cotangent[:, cols - ASIDE:]
    return pl.pallas_call(
        functools.partial(aside_kernel, inv_tokens),
        out_shape=jax.ShapeDtypeStruct(
            (nz, ny, 4 * rows, ASIDE + cols // (4 * ny)), jnp.bfloat16
        ),
        in_specs=[VMEM] * 4,
        out_specs=VMEM,
        scratch_shapes=[pltpu.VMEM((nz, ny, 2 * rows, ASIDE), jnp.float32)],
        compiler_params=PARAMS,
        name="aside",
    )(context, left, right, weight)


def arrival_kernel(value_ref, sum_ref, weight_ref):
    nz, ny, lines, width = value_ref.shape
    rows = lines // 4
    size = width - ASIDE
    total = value_ref[0, :, :, :ASIDE].astype(jnp.float32)
    for z in range(1, nz):
        total = total + value_ref[z, :, :, :ASIDE].astype(jnp.float32)
    sum_ref[...] = total[:, :2 * rows] + total[:, 2 * rows:]
    for y in range(ny):
        part = value_ref[:, y, :, ASIDE:].astype(jnp.float32)
        for q in range(4):
            start = (y * 4 + q) * size
            block = part[:, q * rows:(q + 1) * rows].reshape(nz * rows, size)
            weight_ref[:, start:start + size] = block.astype(jnp.bfloat16)


def arrival(value):
    nz, ny, lines, width = value.shape
    return pl.pallas_call(
        arrival_kernel,
        out_shape=(
            jax.ShapeDtypeStruct((ny, lines // 2, ASIDE), jnp.float32),
            jax.ShapeDtypeStruct((nz * lines // 4, 4 * ny * (width - ASIDE)), jnp.bfloat16),
        ),
        in_specs=[VMEM],
        out_specs=(VMEM,) * 2,
        compiler_params=PARAMS,
        name="arrival",
    )(value)


def sums_kernel(pieces_ref, aside_ref, state_ref, grad_ref, row_ref, packed_ref):
    most = jnp.sum(pieces_ref[...], axis=0)
    width = most.shape[1] - LANES
    grad = jnp.concatenate([most[:, :width], jnp.sum(aside_ref[...], axis=0)], axis=1)
    grad_ref[...] = grad
    lines = packed_ref.shape[1] // 2
    packed_ref[:, lines:, :] = jnp.broadcast_to(most[None, :lines, width:], (packed_ref.shape[0], lines, LANES))
    rows = grad.shape[0] // 2
    plain = grad * grad
    squared = plain + EPS1
    row_sum = jnp.sum(squared, axis=1, keepdims=True)
    row_new = BETA * state_ref[...] + (1.0 - BETA) * (row_sum[:rows] + row_sum[rows:])
    row_ref[...] = row_new
    ratio = plain * (1.0 / jnp.concatenate([row_new, row_new], axis=0))
    per_half = grad.shape[1] // LANES
    for which, value in enumerate((squared, ratio)):
        for half in range(2):
            total = jnp.sum(value[half * rows:(half + 1) * rows], axis=0, keepdims=True)
            for i in range(per_half):
                place = (2 * which + half) * per_half + i
                group, line = divmod(place, lines)
                packed_ref[group, line:line + 1, :] = total[:, i * LANES:(i + 1) * LANES]


def sums_of(pieces, aside, row_state, peers):
    rows, cols = pieces.shape[1], pieces.shape[2] - LANES + ASIDE
    return pl.pallas_call(
        sums_kernel,
        out_shape=(
            jax.ShapeDtypeStruct((rows, cols), jnp.float32),
            jax.ShapeDtypeStruct(row_state.shape, jnp.float32),
            jax.ShapeDtypeStruct((peers, 2 * 4 * cols // (peers * LANES), LANES), jnp.float32),
        ),
        in_specs=[VMEM] * 3,
        out_specs=(VMEM,) * 3,
        compiler_params=PARAMS,
        name="sums",
    )(pieces, aside, row_state)


def update_kernel(entries, sums_ref, total_ref, grad_ref, row_ref, state_ref, out_ref, col_ref, rms_ref):
    groups = col_ref.shape[0]
    total = jnp.sum(jnp.sum(sums_ref[:groups], axis=0, keepdims=True), axis=1, keepdims=True)
    total = BETA * total_ref[:1, :1] + (1.0 - BETA) * total
    col_new = BETA * state_ref[...] + (1.0 - BETA) * sums_ref[:groups]
    col_ref[...] = col_new
    ratio = sums_ref[groups:] / col_new
    ratio = jnp.sum(jnp.sum(ratio, axis=0, keepdims=True), axis=1, keepdims=True)
    rms = jnp.sqrt(total * ratio / entries)
    rms_ref[...] = rms
    clip = jnp.maximum(CLIP, rms)
    rows = row_ref.shape[0]
    row = row_ref[...]
    for i in range(groups):
        half, start = divmod(i, groups // 2)
        start *= LANES
        grad = grad_ref[half * rows:(half + 1) * rows, start:start + LANES]
        scaled = grad / jnp.sqrt(row * col_new[i:i + 1] / total)
        out_ref[:, i * LANES:(i + 1) * LANES] = scaled / clip


def update_of(sums, total, grad, row_new, state, entries):
    rows, cols = row_new.shape[0], 2 * grad.shape[1]
    return pl.pallas_call(
        functools.partial(update_kernel, entries),
        out_shape=(
            jax.ShapeDtypeStruct((rows, cols), jnp.float32),
            jax.ShapeDtypeStruct(state.shape, jnp.float32),
            jax.ShapeDtypeStruct((1, 1), jnp.float32),
        ),
        in_specs=[VMEM] * 5,
        out_specs=(VMEM,) * 3,
        compiler_params=PARAMS,
        name="update",
    )(sums, total, grad, row_new, state)


def fold_kernel(value_ref, out_ref):
    total = jnp.sum(value_ref[...], axis=0, keepdims=True)
    out_ref[...] = jnp.broadcast_to(total, out_ref.shape)


def fold(value, copies):
    return pl.pallas_call(
        fold_kernel,
        out_shape=jax.ShapeDtypeStruct((copies,) + value.shape[1:], value.dtype),
        in_specs=[VMEM],
        out_specs=VMEM,
        compiler_params=PARAMS,
        name="fold",
    )(value)


def split_kernel(value_ref, out_ref, rest_ref):
    total = jnp.sum(value_ref[...], axis=0, keepdims=True)
    lines = out_ref.shape[1]
    out_ref[...] = jnp.broadcast_to(total[:, :lines], out_ref.shape)
    rest_ref[...] = total[0, lines:]


def split_fold(value, copies):
    lines = value.shape[1] // 2
    return pl.pallas_call(
        split_kernel,
        out_shape=(
            jax.ShapeDtypeStruct((copies, lines, LANES), value.dtype),
            jax.ShapeDtypeStruct((lines, LANES), value.dtype),
        ),
        in_specs=[VMEM],
        out_specs=(VMEM,) * 2,
        compiler_params=PARAMS,
        name="split_fold",
    )(value)


def exchange(value, axes):
    return lax.all_to_all(value, axes, 0, 0, tiled=True)


def on_device(context, cotangent, master_weight, row_state, col_state):
    ny, nz = lax.axis_size("y"), lax.axis_size("z")
    nmp = lax.axis_size("x") * lax.axis_size("c")
    rows, cols = master_weight.shape
    inv_tokens = 1.0 / (cotangent.shape[0] * ny * nz)
    entries = rows * ny * nz * nmp * cols

    term = term_of(context, cotangent, row_state, inv_tokens, ny * nz, rows)
    part = lax.psum_scatter(
        term.reshape(ny * nz * 2 * rows, term.shape[2]), "y", scatter_dimension=0, tiled=True
    )
    context, _ = lax.optimization_barrier((context, term))
    aside = aside_of(context, cotangent, master_weight, inv_tokens, ny, nz)
    aside, weight_rows = arrival(exchange(aside, "z"))
    aside = exchange(aside, "y")
    weight_rows, part, aside = lax.optimization_barrier((weight_rows, part, aside))
    weight = lax.all_gather(weight_rows, "y", axis=0, tiled=True)
    grad_input = lax.dot_general(
        cotangent, weight, (((1,), (1,)), ((), ())), preferred_element_type=jnp.float32
    ).astype(jnp.bfloat16)

    pieces = exchange(part.reshape(nz, 2 * rows, term.shape[2]), "z")
    grad, row_new, packed = sums_of(pieces, aside, row_state[:, None], nmp)
    packed, state_sum = split_fold(exchange(packed, NEAR), ny * nz)
    packed = fold(exchange(packed, FAR), nmp)
    packed = exchange(packed, NEAR).reshape(2 * cols // LANES, LANES)
    packed, grad_input = lax.optimization_barrier((packed, grad_input))
    update, col_new, update_rms = update_of(
        packed, state_sum, grad, row_new, col_state.reshape(cols // LANES, LANES), entries
    )
    return (grad_input, update, row_new[:, 0], col_new.reshape(cols), update_rms[0, 0])


def solution(mesh):
    grid = Mesh(mesh.devices.reshape(8, 8, 4, 2), ("y", "z", "x", "c"))
    dp, mp = ("y", "z"), ("x", "c")
    in_specs = (P(dp, mp), P(dp, None), P(mp + dp, None), P(mp + dp), P())
    out_specs = (P(dp, mp), P(mp + dp, None), P(mp + dp), P(), P())
    return jax.shard_map(
        on_device, mesh=grid, in_specs=in_specs, out_specs=out_specs, check_vma=False
    )
```

```python
import functools

import jax
import jax.numpy as jnp
from jax import lax
from jax.experimental import pallas as pl
from jax.experimental.pallas import tpu as pltpu
from jax.sharding import Mesh, PartitionSpec as P

BETA = 0.8
EPS1 = 1e-30
CLIP = 1.0
CHUNK = 768
ASIDE = 512
LANES = 128
NEAR = ("x", "c")
FAR = ("y", "z")
VMEM = pl.BlockSpec(memory_space=pltpu.VMEM)
PARAMS = pltpu.CompilerParams(vmem_limit_bytes=32 * 2**20)


def spans(start, stop):
    return [(i, min(CHUNK, stop - i)) for i in range(start, stop, CHUNK)]


def product(context, cotangent, inv_tokens):
    return inv_tokens * jnp.dot(context, cotangent, preferred_element_type=jnp.float32)


def term_kernel(inv_tokens, context_hbm, cotangent_hbm, out_hbm, context_ref, cotangent_ref, out_ref, in_sems, out_sems):
    peers, rows, width = out_ref.shape[0], out_ref.shape[1] // 2, out_ref.shape[2]
    half_cols = cotangent_hbm.shape[1] // 2
    first = pltpu.make_async_copy(context_hbm, context_ref, in_sems.at[0])
    first.start()
    loads = []
    for k, (start, size) in enumerate(spans(0, width)):
        for half in range(2):
            place = pl.ds(half * half_cols + start, size)
            copy = pltpu.make_async_copy(
                cotangent_hbm.at[:, place], cotangent_ref.at[:, place], in_sems.at[1 + 2 * k + half]
            )
            copy.start()
            loads.append(copy)
    first.wait()
    context = context_ref[...].T
    stores = []
    for k, (start, size) in enumerate(spans(0, width)):
        for half in range(2):
            loads[2 * k + half].wait()
            place = half * half_cols + start
            term = product(context, cotangent_ref[:, place:place + size], inv_tokens)
            out_ref[:, half * rows:(half + 1) * rows, start:start + size] = term.reshape(
                peers, rows, size
            )
        place = pl.ds(start, size)
        copy = pltpu.make_async_copy(
            out_ref.at[:, :, place], out_hbm.at[:, :, place], out_sems.at[k]
        )
        copy.start()
        stores.append(copy)
    for copy in stores:
        copy.wait()


def term_of(context, cotangent, inv_tokens, peers, rows):
    tokens, cols = cotangent.shape
    width = cols // 2 - ASIDE
    count = len(spans(0, width))
    return pl.pallas_call(
        functools.partial(term_kernel, inv_tokens),
        out_shape=jax.ShapeDtypeStruct((peers, 2 * rows, width), jnp.float32),
        in_specs=[pl.BlockSpec(memory_space=pl.ANY)] * 2,
        out_specs=pl.BlockSpec(memory_space=pl.ANY),
        scratch_shapes=[
            pltpu.VMEM(context.shape, context.dtype),
            pltpu.VMEM(cotangent.shape, cotangent.dtype),
            pltpu.VMEM((peers, 2 * rows, width), jnp.float32),
            pltpu.SemaphoreType.DMA((1 + 2 * count,)),
            pltpu.SemaphoreType.DMA((count,)),
        ],
        compiler_params=pltpu.CompilerParams(vmem_limit_bytes=60 * 2**20),
        cost_estimate=pl.CostEstimate(
            flops=2 * tokens * context.shape[1] * cols,
            bytes_accessed=2 * tokens * cols + 4 * peers * rows * cols,
            transcendentals=0,
        ),
        name="term",
    )(context, cotangent)


def aside_kernel(inv_tokens, context_ref, left_ref, right_ref, weight_ref, out_ref, term_ref):
    nz, ny, rows, _ = term_ref.shape
    rows //= 2
    context = context_ref[...].T
    for half, cotangent_ref in enumerate((left_ref, right_ref)):
        term = product(context, cotangent_ref[...], inv_tokens)
        for y in range(ny):
            part = term[y * nz * rows:(y + 1) * nz * rows]
            term_ref[:, y, half * rows:(half + 1) * rows, :] = part.reshape(nz, rows, ASIDE)
    for z in range(nz):
        term = term_ref[z]
        upper = term.astype(jnp.bfloat16).astype(jnp.float32)
        both = jnp.concatenate([upper, term - upper], axis=1)
        out_ref[z, :, :, :ASIDE] = both.astype(jnp.bfloat16)
    size = out_ref.shape[3] - ASIDE
    groups = out_ref.shape[2] // rows
    for y in range(ny):
        starts = [(y * groups + q) * size for q in range(groups)]
        part = jnp.concatenate([weight_ref[:, i:i + size] for i in starts], axis=0)
        out_ref[:, y, :, ASIDE:] = jnp.broadcast_to(part[None], (nz,) + part.shape).astype(
            jnp.bfloat16
        )


def aside_of(context, cotangent, weight, inv_tokens, ny, nz):
    rows, cols = weight.shape
    left = cotangent[:, cols // 2 - ASIDE:cols // 2]
    right = cotangent[:, cols - ASIDE:]
    return pl.pallas_call(
        functools.partial(aside_kernel, inv_tokens),
        out_shape=jax.ShapeDtypeStruct(
            (nz, ny, 4 * rows, ASIDE + cols // (4 * ny)), jnp.bfloat16
        ),
        in_specs=[VMEM] * 4,
        out_specs=VMEM,
        scratch_shapes=[pltpu.VMEM((nz, ny, 2 * rows, ASIDE), jnp.float32)],
        compiler_params=PARAMS,
        name="aside",
    )(context, left, right, weight)


def arrival_kernel(value_ref, sum_ref, weight_ref):
    nz, ny, lines, width = value_ref.shape
    rows = lines // 4
    size = width - ASIDE
    total = value_ref[0, :, :, :ASIDE].astype(jnp.float32)
    for z in range(1, nz):
        total = total + value_ref[z, :, :, :ASIDE].astype(jnp.float32)
    sum_ref[...] = total[:, :2 * rows] + total[:, 2 * rows:]
    for y in range(ny):
        part = value_ref[:, y, :, ASIDE:].astype(jnp.float32)
        for q in range(4):
            start = (y * 4 + q) * size
            block = part[:, q * rows:(q + 1) * rows].reshape(nz * rows, size)
            weight_ref[:, start:start + size] = block.astype(jnp.bfloat16)


def arrival(value):
    nz, ny, lines, width = value.shape
    return pl.pallas_call(
        arrival_kernel,
        out_shape=(
            jax.ShapeDtypeStruct((ny, lines // 2, ASIDE), jnp.float32),
            jax.ShapeDtypeStruct((nz * lines // 4, 4 * ny * (width - ASIDE)), jnp.bfloat16),
        ),
        in_specs=[VMEM],
        out_specs=(VMEM,) * 2,
        compiler_params=PARAMS,
        name="arrival",
    )(value)


def sums_kernel(pieces_ref, aside_ref, state_ref, grad_ref, row_ref, packed_ref):
    grad = jnp.concatenate(
        [jnp.sum(pieces_ref[...], axis=0), jnp.sum(aside_ref[...], axis=0)], axis=1
    )
    grad_ref[...] = grad
    peers, _, size = packed_ref.shape
    lines = size // LANES - 1
    state_sum = jnp.sum(state_ref[...], axis=0, keepdims=True).reshape(1, 1, 1)
    packed_ref[:, :, lines * LANES:] = jnp.broadcast_to(state_sum, (peers, 1, LANES))
    rows = grad.shape[0] // 2
    plain = grad * grad
    squared = plain + EPS1
    row_sum = jnp.sum(squared, axis=1, keepdims=True)
    row_new = BETA * state_ref[...] + (1.0 - BETA) * (row_sum[:rows] + row_sum[rows:])
    row_ref[...] = row_new
    ratio = plain * (1.0 / jnp.concatenate([row_new, row_new], axis=0))
    per_half = grad.shape[1] // LANES
    for which, value in enumerate((squared, ratio)):
        for half in range(2):
            total = jnp.sum(value[half * rows:(half + 1) * rows], axis=0, keepdims=True)
            for i in range(per_half):
                place = (2 * which + half) * per_half + i
                group, line = divmod(place, lines)
                packed_ref[group, :, line * LANES:(line + 1) * LANES] = total[:, i * LANES:(i + 1) * LANES]


def sums_of(pieces, aside, row_state, peers):
    rows, cols = pieces.shape[1], pieces.shape[2] + ASIDE
    return pl.pallas_call(
        sums_kernel,
        out_shape=(
            jax.ShapeDtypeStruct((rows, cols), jnp.float32),
            jax.ShapeDtypeStruct(row_state.shape, jnp.float32),
            jax.ShapeDtypeStruct((peers, 1, 4 * cols // peers + LANES), jnp.float32),
        ),
        in_specs=[VMEM] * 3,
        out_specs=(VMEM,) * 3,
        compiler_params=PARAMS,
        name="sums",
    )(pieces, aside, row_state)


def update_kernel(entries, sums_ref, total_ref, grad_ref, row_ref, state_ref, out_ref, col_ref, rms_ref):
    groups = col_ref.shape[0]
    total = jnp.sum(jnp.sum(sums_ref[:groups], axis=0, keepdims=True), axis=1, keepdims=True)
    total = BETA * total_ref[:1, :1] + (1.0 - BETA) * total
    col_new = BETA * state_ref[...] + (1.0 - BETA) * sums_ref[:groups]
    col_ref[...] = col_new
    ratio = sums_ref[groups:] / col_new
    ratio = jnp.sum(jnp.sum(ratio, axis=0, keepdims=True), axis=1, keepdims=True)
    rms = jnp.sqrt(total * ratio / entries)
    rms_ref[...] = rms
    clip = jnp.maximum(CLIP, rms)
    rows = row_ref.shape[0]
    row = row_ref[...]
    for i in range(groups):
        half, start = divmod(i, groups // 2)
        start *= LANES
        grad = grad_ref[half * rows:(half + 1) * rows, start:start + LANES]
        scaled = grad / jnp.sqrt(row * col_new[i:i + 1] / total)
        out_ref[:, i * LANES:(i + 1) * LANES] = scaled / clip


def update_of(sums, total, grad, row_new, state, entries):
    rows, cols = row_new.shape[0], 2 * grad.shape[1]
    return pl.pallas_call(
        functools.partial(update_kernel, entries),
        out_shape=(
            jax.ShapeDtypeStruct((rows, cols), jnp.float32),
            jax.ShapeDtypeStruct(state.shape, jnp.float32),
            jax.ShapeDtypeStruct((1, 1), jnp.float32),
        ),
        in_specs=[VMEM] * 5,
        out_specs=(VMEM,) * 3,
        compiler_params=PARAMS,
        name="update",
    )(sums, total, grad, row_new, state)


def fold_kernel(value_ref, out_ref):
    total = jnp.sum(value_ref[...], axis=0, keepdims=True)
    out_ref[...] = jnp.broadcast_to(total, out_ref.shape)


def fold(value, copies):
    return pl.pallas_call(
        fold_kernel,
        out_shape=jax.ShapeDtypeStruct((copies,) + value.shape[1:], value.dtype),
        in_specs=[VMEM],
        out_specs=VMEM,
        compiler_params=PARAMS,
        name="fold",
    )(value)


def exchange(value, axes):
    return lax.all_to_all(value, axes, 0, 0, tiled=True)


def on_device(context, cotangent, master_weight, row_state, col_state):
    ny, nz = lax.axis_size("y"), lax.axis_size("z")
    nmp = lax.axis_size("x") * lax.axis_size("c")
    rows, cols = master_weight.shape
    inv_tokens = 1.0 / (cotangent.shape[0] * ny * nz)
    entries = rows * ny * nz * nmp * cols

    term = term_of(context, cotangent, inv_tokens, ny * nz, rows)
    part = lax.psum_scatter(
        term.reshape(ny * nz * 2 * rows, term.shape[2]), "y", scatter_dimension=0, tiled=True
    )
    context, _ = lax.optimization_barrier((context, term))
    aside = aside_of(context, cotangent, master_weight, inv_tokens, ny, nz)
    aside, weight_rows = arrival(exchange(aside, "z"))
    aside = exchange(aside, "y")
    weight_rows, part, aside = lax.optimization_barrier((weight_rows, part, aside))
    weight = lax.all_gather(weight_rows, "y", axis=0, tiled=True)
    grad_input = lax.dot_general(
        cotangent, weight, (((1,), (1,)), ((), ())), preferred_element_type=jnp.float32
    ).astype(jnp.bfloat16)

    pieces = exchange(part.reshape(nz, 2 * rows, term.shape[2]), "z")
    grad, row_new, packed = sums_of(pieces, aside, row_state[:, None], nmp)
    packed = fold(exchange(packed, NEAR), ny * nz)
    packed = fold(exchange(packed, FAR), nmp)
    state_sum = packed[0, :, packed.shape[2] - LANES:]
    packed = exchange(packed[:, :, :packed.shape[2] - LANES], NEAR)
    packed = packed.reshape(2 * cols // LANES, LANES)
    packed, grad_input = lax.optimization_barrier((packed, grad_input))
    update, col_new, update_rms = update_of(
        packed, state_sum, grad, row_new, col_state.reshape(cols // LANES, LANES), entries
    )
    return (grad_input, update, row_new[:, 0], col_new.reshape(cols), update_rms[0, 0])


def solution(mesh):
    grid = Mesh(mesh.devices.reshape(8, 8, 4, 2), ("y", "z", "x", "c"))
    dp, mp = ("y", "z"), ("x", "c")
    in_specs = (P(dp, mp), P(dp, None), P(mp + dp, None), P(mp + dp), P())
    out_specs = (P(dp, mp), P(mp + dp, None), P(mp + dp), P(), P())
    return jax.shard_map(
        on_device, mesh=grid, in_specs=in_specs, out_specs=out_specs, check_vma=False
    )
```

```python
import functools

import jax
import jax.numpy as jnp
from jax import lax
from jax.experimental import pallas as pl
from jax.experimental.pallas import tpu as pltpu
from jax.sharding import Mesh, PartitionSpec as P

BETA = 0.8
EPS1 = 1e-30
CLIP = 1.0
CHUNK = 768
ASIDE = 512
LANES = 128
NEAR = ("x", "c")
VMEM = pl.BlockSpec(memory_space=pltpu.VMEM)
PARAMS = pltpu.CompilerParams(vmem_limit_bytes=32 * 2**20)


def spans(start, stop):
    return [(i, min(CHUNK, stop - i)) for i in range(start, stop, CHUNK)]


def product(context, cotangent, inv_tokens):
    return inv_tokens * jnp.dot(context, cotangent, preferred_element_type=jnp.float32)


def term_kernel(inv_tokens, context_hbm, cotangent_hbm, out_hbm, context_ref, cotangent_ref, out_ref, in_sems, out_sems):
    peers, rows, width = out_ref.shape[0], out_ref.shape[1] // 2, out_ref.shape[2]
    half_cols = cotangent_hbm.shape[1] // 2
    first = pltpu.make_async_copy(context_hbm, context_ref, in_sems.at[0])
    first.start()
    loads = []
    for k, (start, size) in enumerate(spans(0, width)):
        for half in range(2):
            place = pl.ds(half * half_cols + start, size)
            copy = pltpu.make_async_copy(
                cotangent_hbm.at[:, place], cotangent_ref.at[:, place], in_sems.at[1 + 2 * k + half]
            )
            copy.start()
            loads.append(copy)
    first.wait()
    context = context_ref[...].T
    stores = []
    for k, (start, size) in enumerate(spans(0, width)):
        for half in range(2):
            loads[2 * k + half].wait()
            place = half * half_cols + start
            term = product(context, cotangent_ref[:, place:place + size], inv_tokens)
            out_ref[:, half * rows:(half + 1) * rows, start:start + size] = term.reshape(
                peers, rows, size
            )
        place = pl.ds(start, size)
        copy = pltpu.make_async_copy(
            out_ref.at[:, :, place], out_hbm.at[:, :, place], out_sems.at[k]
        )
        copy.start()
        stores.append(copy)
    for copy in stores:
        copy.wait()


def term_of(context, cotangent, inv_tokens, peers, rows):
    tokens, cols = cotangent.shape
    width = cols // 2 - ASIDE
    count = len(spans(0, width))
    return pl.pallas_call(
        functools.partial(term_kernel, inv_tokens),
        out_shape=jax.ShapeDtypeStruct((peers, 2 * rows, width), jnp.float32),
        in_specs=[pl.BlockSpec(memory_space=pl.ANY)] * 2,
        out_specs=pl.BlockSpec(memory_space=pl.ANY),
        scratch_shapes=[
            pltpu.VMEM(context.shape, context.dtype),
            pltpu.VMEM(cotangent.shape, cotangent.dtype),
            pltpu.VMEM((peers, 2 * rows, width), jnp.float32),
            pltpu.SemaphoreType.DMA((1 + 2 * count,)),
            pltpu.SemaphoreType.DMA((count,)),
        ],
        compiler_params=pltpu.CompilerParams(vmem_limit_bytes=60 * 2**20),
        cost_estimate=pl.CostEstimate(
            flops=2 * tokens * context.shape[1] * cols,
            bytes_accessed=2 * tokens * cols + 4 * peers * rows * cols,
            transcendentals=0,
        ),
        name="term",
    )(context, cotangent)


def aside_kernel(inv_tokens, context_ref, left_ref, right_ref, weight_ref, out_ref, term_ref):
    nz, ny, rows, _ = term_ref.shape
    rows //= 2
    context = context_ref[...].T
    for half, cotangent_ref in enumerate((left_ref, right_ref)):
        term = product(context, cotangent_ref[...], inv_tokens)
        for y in range(ny):
            part = term[y * nz * rows:(y + 1) * nz * rows]
            term_ref[:, y, half * rows:(half + 1) * rows, :] = part.reshape(nz, rows, ASIDE)
    for z in range(nz):
        term = term_ref[z]
        upper = term.astype(jnp.bfloat16).astype(jnp.float32)
        both = jnp.concatenate([upper, term - upper], axis=1)
        out_ref[z, :, :, :ASIDE] = both.astype(jnp.bfloat16)
    size = out_ref.shape[3] - ASIDE
    groups = out_ref.shape[2] // rows
    for y in range(ny):
        starts = [(y * groups + q) * size for q in range(groups)]
        part = jnp.concatenate([weight_ref[:, i:i + size] for i in starts], axis=0)
        out_ref[:, y, :, ASIDE:] = jnp.broadcast_to(part[None], (nz,) + part.shape).astype(
            jnp.bfloat16
        )


def aside_of(context, cotangent, weight, inv_tokens, ny, nz):
    rows, cols = weight.shape
    left = cotangent[:, cols // 2 - ASIDE:cols // 2]
    right = cotangent[:, cols - ASIDE:]
    return pl.pallas_call(
        functools.partial(aside_kernel, inv_tokens),
        out_shape=jax.ShapeDtypeStruct(
            (nz, ny, 4 * rows, ASIDE + cols // (4 * ny)), jnp.bfloat16
        ),
        in_specs=[VMEM] * 4,
        out_specs=VMEM,
        scratch_shapes=[pltpu.VMEM((nz, ny, 2 * rows, ASIDE), jnp.float32)],
        compiler_params=PARAMS,
        name="aside",
    )(context, left, right, weight)


def arrival_kernel(value_ref, sum_ref, weight_ref):
    nz, ny, lines, width = value_ref.shape
    rows = lines // 4
    size = width - ASIDE
    total = value_ref[0, :, :, :ASIDE].astype(jnp.float32)
    for z in range(1, nz):
        total = total + value_ref[z, :, :, :ASIDE].astype(jnp.float32)
    sum_ref[...] = total[:, :2 * rows] + total[:, 2 * rows:]
    for y in range(ny):
        part = value_ref[:, y, :, ASIDE:].astype(jnp.float32)
        for q in range(4):
            start = (y * 4 + q) * size
            block = part[:, q * rows:(q + 1) * rows].reshape(nz * rows, size)
            weight_ref[:, start:start + size] = block.astype(jnp.bfloat16)


def arrival(value):
    nz, ny, lines, width = value.shape
    return pl.pallas_call(
        arrival_kernel,
        out_shape=(
            jax.ShapeDtypeStruct((ny, lines // 2, ASIDE), jnp.float32),
            jax.ShapeDtypeStruct((nz * lines // 4, 4 * ny * (width - ASIDE)), jnp.bfloat16),
        ),
        in_specs=[VMEM],
        out_specs=(VMEM,) * 2,
        compiler_params=PARAMS,
        name="arrival",
    )(value)


def sums_kernel(pieces_ref, aside_ref, state_ref, grad_ref, row_ref, packed_ref):
    grad = jnp.concatenate(
        [jnp.sum(pieces_ref[...], axis=0), jnp.sum(aside_ref[...], axis=0)], axis=1
    )
    grad_ref[...] = grad
    peers, _, size = packed_ref.shape
    lines = size // LANES - 1
    state_sum = jnp.sum(state_ref[...], axis=0, keepdims=True).reshape(1, 1, 1)
    packed_ref[:, :, lines * LANES:] = jnp.broadcast_to(state_sum, (peers, 1, LANES))
    rows = grad.shape[0] // 2
    plain = grad * grad
    squared = plain + EPS1
    row_sum = jnp.sum(squared, axis=1, keepdims=True)
    row_new = BETA * state_ref[...] + (1.0 - BETA) * (row_sum[:rows] + row_sum[rows:])
    row_ref[...] = row_new
    ratio = plain * (1.0 / jnp.concatenate([row_new, row_new], axis=0))
    per_half = grad.shape[1] // LANES
    for which, value in enumerate((squared, ratio)):
        for half in range(2):
            total = jnp.sum(value[half * rows:(half + 1) * rows], axis=0, keepdims=True)
            for i in range(per_half):
                place = (2 * which + half) * per_half + i
                group, line = divmod(place, lines)
                packed_ref[group, :, line * LANES:(line + 1) * LANES] = total[:, i * LANES:(i + 1) * LANES]


def sums_of(pieces, aside, row_state, peers):
    rows, cols = pieces.shape[1], pieces.shape[2] + ASIDE
    return pl.pallas_call(
        sums_kernel,
        out_shape=(
            jax.ShapeDtypeStruct((rows, cols), jnp.float32),
            jax.ShapeDtypeStruct(row_state.shape, jnp.float32),
            jax.ShapeDtypeStruct((peers, 1, 4 * cols // peers + LANES), jnp.float32),
        ),
        in_specs=[VMEM] * 3,
        out_specs=(VMEM,) * 3,
        compiler_params=PARAMS,
        name="sums",
    )(pieces, aside, row_state)


def update_kernel(entries, sums_ref, total_ref, grad_ref, row_ref, state_ref, out_ref, col_ref, rms_ref):
    groups = col_ref.shape[0]
    total = jnp.sum(jnp.sum(sums_ref[:groups], axis=0, keepdims=True), axis=1, keepdims=True)
    total = BETA * total_ref[:1, :1] + (1.0 - BETA) * total
    col_new = BETA * state_ref[...] + (1.0 - BETA) * sums_ref[:groups]
    col_ref[...] = col_new
    ratio = sums_ref[groups:] / col_new
    ratio = jnp.sum(jnp.sum(ratio, axis=0, keepdims=True), axis=1, keepdims=True)
    rms = jnp.sqrt(total * ratio / entries)
    rms_ref[...] = rms
    clip = jnp.maximum(CLIP, rms)
    rows = row_ref.shape[0]
    row = row_ref[...]
    for i in range(groups):
        half, start = divmod(i, groups // 2)
        start *= LANES
        grad = grad_ref[half * rows:(half + 1) * rows, start:start + LANES]
        scaled = grad / jnp.sqrt(row * col_new[i:i + 1] / total)
        out_ref[:, i * LANES:(i + 1) * LANES] = scaled / clip


def update_of(sums, total, grad, row_new, state, entries):
    rows, cols = row_new.shape[0], 2 * grad.shape[1]
    return pl.pallas_call(
        functools.partial(update_kernel, entries),
        out_shape=(
            jax.ShapeDtypeStruct((rows, cols), jnp.float32),
            jax.ShapeDtypeStruct(state.shape, jnp.float32),
            jax.ShapeDtypeStruct((1, 1), jnp.float32),
        ),
        in_specs=[VMEM] * 5,
        out_specs=(VMEM,) * 3,
        compiler_params=PARAMS,
        name="update",
    )(sums, total, grad, row_new, state)


def fold_kernel(value_ref, out_ref):
    total = jnp.sum(value_ref[...], axis=0, keepdims=True)
    out_ref[...] = jnp.broadcast_to(total, out_ref.shape)


def fold(value, copies):
    return pl.pallas_call(
        fold_kernel,
        out_shape=jax.ShapeDtypeStruct((copies,) + value.shape[1:], value.dtype),
        in_specs=[VMEM],
        out_specs=VMEM,
        compiler_params=PARAMS,
        name="fold",
    )(value)


def split_kernel(value_ref, out_ref, last_ref):
    total = jnp.sum(value_ref[...], axis=0, keepdims=True)
    size = out_ref.shape[2]
    out_ref[...] = jnp.broadcast_to(total[:, :, :size], out_ref.shape)
    last_ref[...] = total[0, :, size:]


def split_fold(value, copies):
    size = value.shape[2] - LANES
    return pl.pallas_call(
        split_kernel,
        out_shape=(
            jax.ShapeDtypeStruct((copies, 1, size), value.dtype),
            jax.ShapeDtypeStruct((1, LANES), value.dtype),
        ),
        in_specs=[VMEM],
        out_specs=(VMEM,) * 2,
        compiler_params=PARAMS,
        name="split_fold",
    )(value)


def exchange(value, axes):
    return lax.all_to_all(value, axes, 0, 0, tiled=True)


def on_device(context, cotangent, master_weight, row_state, col_state):
    ny, nz = lax.axis_size("y"), lax.axis_size("z")
    nmp = lax.axis_size("x") * lax.axis_size("c")
    rows, cols = master_weight.shape
    inv_tokens = 1.0 / (cotangent.shape[0] * ny * nz)
    entries = rows * ny * nz * nmp * cols

    term = term_of(context, cotangent, inv_tokens, ny * nz, rows)
    part = lax.psum_scatter(
        term.reshape(ny * nz * 2 * rows, term.shape[2]), "y", scatter_dimension=0, tiled=True
    )
    context, _ = lax.optimization_barrier((context, term))
    aside = aside_of(context, cotangent, master_weight, inv_tokens, ny, nz)
    aside, weight_rows = arrival(exchange(aside, "z"))
    aside = exchange(aside, "y")
    weight_rows, part, aside = lax.optimization_barrier((weight_rows, part, aside))
    weight = lax.all_gather(weight_rows, "y", axis=0, tiled=True)
    grad_input = lax.dot_general(
        cotangent, weight, (((1,), (1,)), ((), ())), preferred_element_type=jnp.float32
    ).astype(jnp.bfloat16)

    pieces = exchange(part.reshape(nz, 2 * rows, term.shape[2]), "z")
    grad, row_new, packed = sums_of(pieces, aside, row_state[:, None], nmp)
    packed = fold(exchange(packed, NEAR), nz)
    packed = fold(exchange(packed, "z"), ny)
    packed, state_sum = split_fold(exchange(packed, "y"), nmp)
    packed = exchange(packed, NEAR).reshape(2 * cols // LANES, LANES)
    packed, grad_input = lax.optimization_barrier((packed, grad_input))
    update, col_new, update_rms = update_of(
        packed, state_sum, grad, row_new, col_state.reshape(cols // LANES, LANES), entries
    )
    return (grad_input, update, row_new[:, 0], col_new.reshape(cols), update_rms[0, 0])


def solution(mesh):
    grid = Mesh(mesh.devices.reshape(8, 8, 4, 2), ("y", "z", "x", "c"))
    dp, mp = ("y", "z"), ("x", "c")
    in_specs = (P(dp, mp), P(dp, None), P(mp + dp, None), P(mp + dp), P())
    out_specs = (P(dp, mp), P(mp + dp, None), P(mp + dp), P(), P())
    return jax.shard_map(
        on_device, mesh=grid, in_specs=in_specs, out_specs=out_specs, check_vma=False
    )
```

```python
import functools

import jax
import jax.numpy as jnp
from jax import lax
from jax.experimental import pallas as pl
from jax.experimental.pallas import tpu as pltpu
from jax.sharding import Mesh, PartitionSpec as P

BETA = 0.8
EPS1 = 1e-30
CLIP = 1.0
CHUNK = 768
ASIDE = 512
LANES = 128
NEAR = ("x", "c")
VMEM = pl.BlockSpec(memory_space=pltpu.VMEM)
PARAMS = pltpu.CompilerParams(vmem_limit_bytes=32 * 2**20)


def spans(start, stop):
    return [(i, min(CHUNK, stop - i)) for i in range(start, stop, CHUNK)]


def product(context, cotangent, inv_tokens):
    return inv_tokens * jnp.dot(context, cotangent, preferred_element_type=jnp.float32)


def term_kernel(inv_tokens, context_hbm, cotangent_hbm, out_hbm, context_ref, cotangent_ref, out_ref, in_sems, out_sems):
    peers, rows, width = out_ref.shape[0], out_ref.shape[1] // 2, out_ref.shape[2]
    half_cols = cotangent_hbm.shape[1] // 2
    first = pltpu.make_async_copy(context_hbm, context_ref, in_sems.at[0])
    first.start()
    loads = []
    for k, (start, size) in enumerate(spans(0, width)):
        for half in range(2):
            place = pl.ds(half * half_cols + start, size)
            copy = pltpu.make_async_copy(
                cotangent_hbm.at[:, place], cotangent_ref.at[:, place], in_sems.at[1 + 2 * k + half]
            )
            copy.start()
            loads.append(copy)
    first.wait()
    context = context_ref[...].T
    stores = []
    for k, (start, size) in enumerate(spans(0, width)):
        for half in range(2):
            loads[2 * k + half].wait()
            place = half * half_cols + start
            term = product(context, cotangent_ref[:, place:place + size], inv_tokens)
            out_ref[:, half * rows:(half + 1) * rows, start:start + size] = term.reshape(
                peers, rows, size
            )
        place = pl.ds(start, size)
        copy = pltpu.make_async_copy(
            out_ref.at[:, :, place], out_hbm.at[:, :, place], out_sems.at[k]
        )
        copy.start()
        stores.append(copy)
    for copy in stores:
        copy.wait()


def term_of(context, cotangent, inv_tokens, peers, rows):
    tokens, cols = cotangent.shape
    width = cols // 2 - ASIDE
    count = len(spans(0, width))
    return pl.pallas_call(
        functools.partial(term_kernel, inv_tokens),
        out_shape=jax.ShapeDtypeStruct((peers, 2 * rows, width), jnp.float32),
        in_specs=[pl.BlockSpec(memory_space=pl.ANY)] * 2,
        out_specs=pl.BlockSpec(memory_space=pl.ANY),
        scratch_shapes=[
            pltpu.VMEM(context.shape, context.dtype),
            pltpu.VMEM(cotangent.shape, cotangent.dtype),
            pltpu.VMEM((peers, 2 * rows, width), jnp.float32),
            pltpu.SemaphoreType.DMA((1 + 2 * count,)),
            pltpu.SemaphoreType.DMA((count,)),
        ],
        compiler_params=pltpu.CompilerParams(vmem_limit_bytes=60 * 2**20),
        cost_estimate=pl.CostEstimate(
            flops=2 * tokens * context.shape[1] * cols,
            bytes_accessed=2 * tokens * cols + 4 * peers * rows * cols,
            transcendentals=0,
        ),
        name="term",
    )(context, cotangent)


def aside_kernel(inv_tokens, context_ref, left_ref, right_ref, weight_ref, out_ref, term_ref):
    nz, ny, rows, _ = term_ref.shape
    rows //= 2
    context = context_ref[...].T
    for half, cotangent_ref in enumerate((left_ref, right_ref)):
        term = product(context, cotangent_ref[...], inv_tokens)
        for y in range(ny):
            part = term[y * nz * rows:(y + 1) * nz * rows]
            term_ref[:, y, half * rows:(half + 1) * rows, :] = part.reshape(nz, rows, ASIDE)
    for z in range(nz):
        term = term_ref[z]
        upper = term.astype(jnp.bfloat16).astype(jnp.float32)
        both = jnp.concatenate([upper, term - upper], axis=1)
        out_ref[z, :, :, :ASIDE] = both.astype(jnp.bfloat16)
    size = out_ref.shape[3] - ASIDE
    groups = out_ref.shape[2] // rows
    for y in range(ny):
        starts = [(y * groups + q) * size for q in range(groups)]
        part = jnp.concatenate([weight_ref[:, i:i + size] for i in starts], axis=0)
        out_ref[:, y, :, ASIDE:] = jnp.broadcast_to(part[None], (nz,) + part.shape).astype(
            jnp.bfloat16
        )


def aside_of(context, cotangent, weight, inv_tokens, ny, nz):
    rows, cols = weight.shape
    left = cotangent[:, cols // 2 - ASIDE:cols // 2]
    right = cotangent[:, cols - ASIDE:]
    return pl.pallas_call(
        functools.partial(aside_kernel, inv_tokens),
        out_shape=jax.ShapeDtypeStruct(
            (nz, ny, 4 * rows, ASIDE + cols // (4 * ny)), jnp.bfloat16
        ),
        in_specs=[VMEM] * 4,
        out_specs=VMEM,
        scratch_shapes=[pltpu.VMEM((nz, ny, 2 * rows, ASIDE), jnp.float32)],
        compiler_params=PARAMS,
        name="aside",
    )(context, left, right, weight)


def arrival_kernel(value_ref, sum_ref, weight_ref):
    nz, ny, lines, width = value_ref.shape
    rows = lines // 4
    size = width - ASIDE
    total = value_ref[0, :, :, :ASIDE].astype(jnp.float32)
    for z in range(1, nz):
        total = total + value_ref[z, :, :, :ASIDE].astype(jnp.float32)
    sum_ref[...] = total[:, :2 * rows] + total[:, 2 * rows:]
    for y in range(ny):
        part = value_ref[:, y, :, ASIDE:].astype(jnp.float32)
        for q in range(4):
            start = (y * 4 + q) * size
            block = part[:, q * rows:(q + 1) * rows].reshape(nz * rows, size)
            weight_ref[:, start:start + size] = block.astype(jnp.bfloat16)


def arrival(value):
    nz, ny, lines, width = value.shape
    return pl.pallas_call(
        arrival_kernel,
        out_shape=(
            jax.ShapeDtypeStruct((ny, lines // 2, ASIDE), jnp.float32),
            jax.ShapeDtypeStruct((nz * lines // 4, 4 * ny * (width - ASIDE)), jnp.bfloat16),
        ),
        in_specs=[VMEM],
        out_specs=(VMEM,) * 2,
        compiler_params=PARAMS,
        name="arrival",
    )(value)


def sums_kernel(pieces_ref, aside_ref, state_ref, grad_ref, row_ref, packed_ref):
    grad = jnp.concatenate(
        [jnp.sum(pieces_ref[...], axis=0), jnp.sum(aside_ref[...], axis=0)], axis=1
    )
    grad_ref[...] = grad
    peers, _, size = packed_ref.shape
    lines = size // LANES - 1
    state_sum = jnp.sum(state_ref[...], axis=0, keepdims=True).reshape(1, 1, 1)
    packed_ref[:, :, lines * LANES:] = jnp.broadcast_to(state_sum, (peers, 1, LANES))
    rows = grad.shape[0] // 2
    plain = grad * grad
    squared = plain + EPS1
    row_sum = jnp.sum(squared, axis=1, keepdims=True)
    row_new = BETA * state_ref[...] + (1.0 - BETA) * (row_sum[:rows] + row_sum[rows:])
    row_ref[...] = row_new
    ratio = plain * (1.0 / jnp.concatenate([row_new, row_new], axis=0))
    per_half = grad.shape[1] // LANES
    for which, value in enumerate((squared, ratio)):
        for half in range(2):
            total = jnp.sum(value[half * rows:(half + 1) * rows], axis=0, keepdims=True)
            for i in range(per_half):
                place = (2 * which + half) * per_half + i
                group, line = divmod(place, lines)
                packed_ref[group, :, line * LANES:(line + 1) * LANES] = total[:, i * LANES:(i + 1) * LANES]


def sums_of(pieces, aside, row_state, peers):
    rows, cols = pieces.shape[1], pieces.shape[2] + ASIDE
    return pl.pallas_call(
        sums_kernel,
        out_shape=(
            jax.ShapeDtypeStruct((rows, cols), jnp.float32),
            jax.ShapeDtypeStruct(row_state.shape, jnp.float32),
            jax.ShapeDtypeStruct((peers, 1, 4 * cols // peers + LANES), jnp.float32),
        ),
        in_specs=[VMEM] * 3,
        out_specs=(VMEM,) * 3,
        compiler_params=PARAMS,
        name="sums",
    )(pieces, aside, row_state)


def update_kernel(entries, sums_ref, total_ref, grad_ref, row_ref, state_ref, out_ref, col_ref, rms_ref):
    groups = col_ref.shape[0]
    total = jnp.sum(jnp.sum(sums_ref[:groups], axis=0, keepdims=True), axis=1, keepdims=True)
    total = BETA * total_ref[:1, :1] + (1.0 - BETA) * total
    col_new = BETA * state_ref[...] + (1.0 - BETA) * sums_ref[:groups]
    col_ref[...] = col_new
    ratio = sums_ref[groups:] / col_new
    ratio = jnp.sum(jnp.sum(ratio, axis=0, keepdims=True), axis=1, keepdims=True)
    rms = jnp.sqrt(total * ratio / entries)
    rms_ref[...] = rms
    clip = jnp.maximum(CLIP, rms)
    rows = row_ref.shape[0]
    row = row_ref[...]
    for i in range(groups):
        half, start = divmod(i, groups // 2)
        start *= LANES
        grad = grad_ref[half * rows:(half + 1) * rows, start:start + LANES]
        scaled = grad / jnp.sqrt(row * col_new[i:i + 1] / total)
        out_ref[:, i * LANES:(i + 1) * LANES] = scaled / clip


def update_of(sums, total, grad, row_new, state, entries):
    rows, cols = row_new.shape[0], 2 * grad.shape[1]
    return pl.pallas_call(
        functools.partial(update_kernel, entries),
        out_shape=(
            jax.ShapeDtypeStruct((rows, cols), jnp.float32),
            jax.ShapeDtypeStruct(state.shape, jnp.float32),
            jax.ShapeDtypeStruct((1, 1), jnp.float32),
        ),
        in_specs=[VMEM] * 5,
        out_specs=(VMEM,) * 3,
        compiler_params=PARAMS,
        name="update",
    )(sums, total, grad, row_new, state)


def fold_kernel(value_ref, out_ref):
    total = jnp.sum(value_ref[...], axis=0, keepdims=True)
    out_ref[...] = jnp.broadcast_to(total, out_ref.shape)


def fold(value, copies):
    return pl.pallas_call(
        fold_kernel,
        out_shape=jax.ShapeDtypeStruct((copies,) + value.shape[1:], value.dtype),
        in_specs=[VMEM],
        out_specs=VMEM,
        compiler_params=PARAMS,
        name="fold",
    )(value)


def split_kernel(value_ref, out_ref, last_ref):
    total = jnp.sum(value_ref[...], axis=0, keepdims=True)
    size = out_ref.shape[2]
    out_ref[...] = jnp.broadcast_to(total[:, :, :size], out_ref.shape)
    last_ref[...] = total[0, :, size:]


def split_fold(value, copies):
    size = value.shape[2] - LANES
    return pl.pallas_call(
        split_kernel,
        out_shape=(
            jax.ShapeDtypeStruct((copies, 1, size), value.dtype),
            jax.ShapeDtypeStruct((1, LANES), value.dtype),
        ),
        in_specs=[VMEM],
        out_specs=(VMEM,) * 2,
        compiler_params=PARAMS,
        name="split_fold",
    )(value)


def exchange(value, axes):
    return lax.all_to_all(value, axes, 0, 0, tiled=True)


def on_device(context, cotangent, master_weight, row_state, col_state):
    ny, nz = lax.axis_size("y"), lax.axis_size("z")
    nmp = lax.axis_size("x") * lax.axis_size("c")
    rows, cols = master_weight.shape
    inv_tokens = 1.0 / (cotangent.shape[0] * ny * nz)
    entries = rows * ny * nz * nmp * cols

    term = term_of(context, cotangent, inv_tokens, ny * nz, rows)
    part = lax.psum_scatter(
        term.reshape(ny * nz * 2 * rows, term.shape[2]), "y", scatter_dimension=0, tiled=True
    )
    context, _ = lax.optimization_barrier((context, term))
    aside = aside_of(context, cotangent, master_weight, inv_tokens, ny, nz)
    aside, weight_rows = arrival(exchange(aside, "z"))
    aside = exchange(aside, "y")
    weight_rows, part, aside = lax.optimization_barrier((weight_rows, part, aside))
    weight = lax.all_gather(weight_rows, "y", axis=0, tiled=True)
    grad_input = lax.dot_general(
        cotangent, weight, (((1,), (1,)), ((), ())), preferred_element_type=jnp.float32
    ).astype(jnp.bfloat16)

    pieces = exchange(part.reshape(nz, 2 * rows, term.shape[2]), "z")
    grad, row_new, packed = sums_of(pieces, aside, row_state[:, None], nmp)
    packed = fold(exchange(packed, NEAR), nz)
    packed = fold(exchange(packed, "z"), ny)
    packed, grad_input = lax.optimization_barrier((exchange(packed, "y"), grad_input))
    packed, state_sum = split_fold(packed, nmp)
    packed = exchange(packed, NEAR).reshape(2 * cols // LANES, LANES)
    update, col_new, update_rms = update_of(
        packed, state_sum, grad, row_new, col_state.reshape(cols // LANES, LANES), entries
    )
    return (grad_input, update, row_new[:, 0], col_new.reshape(cols), update_rms[0, 0])


def solution(mesh):
    grid = Mesh(mesh.devices.reshape(8, 8, 4, 2), ("y", "z", "x", "c"))
    dp, mp = ("y", "z"), ("x", "c")
    in_specs = (P(dp, mp), P(dp, None), P(mp + dp, None), P(mp + dp), P())
    out_specs = (P(dp, mp), P(mp + dp, None), P(mp + dp), P(), P())
    return jax.shard_map(
        on_device, mesh=grid, in_specs=in_specs, out_specs=out_specs, check_vma=False
    )
```

```python
import functools

import jax
import jax.numpy as jnp
from jax import lax
from jax.experimental import pallas as pl
from jax.experimental.pallas import tpu as pltpu
from jax.sharding import Mesh, PartitionSpec as P

BETA = 0.8
EPS1 = 1e-30
CLIP = 1.0
CHUNK = 768
ASIDE = 512
LANES = 128
NEAR = ("x", "c")
FAR = ("y", "z")
VMEM = pl.BlockSpec(memory_space=pltpu.VMEM)
PARAMS = pltpu.CompilerParams(vmem_limit_bytes=32 * 2**20)


def spans(start, stop):
    return [(i, min(CHUNK, stop - i)) for i in range(start, stop, CHUNK)]


def product(context, cotangent, inv_tokens):
    return inv_tokens * jnp.dot(context, cotangent, preferred_element_type=jnp.float32)


def term_kernel(inv_tokens, context_hbm, cotangent_hbm, out_hbm, context_ref, cotangent_ref, out_ref, in_sems, out_sems):
    peers, rows, width = out_ref.shape[0], out_ref.shape[1] // 2, out_ref.shape[2]
    half_cols = cotangent_hbm.shape[1] // 2
    first = pltpu.make_async_copy(context_hbm, context_ref, in_sems.at[0])
    first.start()
    loads = []
    for k, (start, size) in enumerate(spans(0, width)):
        for half in range(2):
            place = pl.ds(half * half_cols + start, size)
            copy = pltpu.make_async_copy(
                cotangent_hbm.at[:, place], cotangent_ref.at[:, place], in_sems.at[1 + 2 * k + half]
            )
            copy.start()
            loads.append(copy)
    first.wait()
    context = context_ref[...].T
    stores = []
    for k, (start, size) in enumerate(spans(0, width)):
        for half in range(2):
            loads[2 * k + half].wait()
            place = half * half_cols + start
            term = product(context, cotangent_ref[:, place:place + size], inv_tokens)
            out_ref[:, half * rows:(half + 1) * rows, start:start + size] = term.reshape(
                peers, rows, size
            )
        place = pl.ds(start, size)
        copy = pltpu.make_async_copy(
            out_ref.at[:, :, place], out_hbm.at[:, :, place], out_sems.at[k]
        )
        copy.start()
        stores.append(copy)
    for copy in stores:
        copy.wait()


def term_of(context, cotangent, inv_tokens, peers, rows):
    tokens, cols = cotangent.shape
    width = cols // 2 - ASIDE
    count = len(spans(0, width))
    return pl.pallas_call(
        functools.partial(term_kernel, inv_tokens),
        out_shape=jax.ShapeDtypeStruct((peers, 2 * rows, width), jnp.float32),
        in_specs=[pl.BlockSpec(memory_space=pl.ANY)] * 2,
        out_specs=pl.BlockSpec(memory_space=pl.ANY),
        scratch_shapes=[
            pltpu.VMEM(context.shape, context.dtype),
            pltpu.VMEM(cotangent.shape, cotangent.dtype),
            pltpu.VMEM((peers, 2 * rows, width), jnp.float32),
            pltpu.SemaphoreType.DMA((1 + 2 * count,)),
            pltpu.SemaphoreType.DMA((count,)),
        ],
        compiler_params=pltpu.CompilerParams(vmem_limit_bytes=60 * 2**20),
        cost_estimate=pl.CostEstimate(
            flops=2 * tokens * context.shape[1] * cols,
            bytes_accessed=2 * tokens * cols + 4 * peers * rows * cols,
            transcendentals=0,
        ),
        name="term",
    )(context, cotangent)


def aside_kernel(inv_tokens, context_ref, left_ref, right_ref, weight_ref, out_ref, term_ref):
    nz, ny, rows, _ = term_ref.shape
    rows //= 2
    context = context_ref[...].T
    for half, cotangent_ref in enumerate((left_ref, right_ref)):
        term = product(context, cotangent_ref[...], inv_tokens)
        for y in range(ny):
            part = term[y * nz * rows:(y + 1) * nz * rows]
            term_ref[:, y, half * rows:(half + 1) * rows, :] = part.reshape(nz, rows, ASIDE)
    for z in range(nz):
        term = term_ref[z]
        upper = term.astype(jnp.bfloat16).astype(jnp.float32)
        both = jnp.concatenate([upper, term - upper], axis=1)
        out_ref[z, :, :, :ASIDE] = both.astype(jnp.bfloat16)
    size = out_ref.shape[3] - ASIDE
    groups = out_ref.shape[2] // rows
    for y in range(ny):
        starts = [(y * groups + q) * size for q in range(groups)]
        part = jnp.concatenate([weight_ref[:, i:i + size] for i in starts], axis=0)
        out_ref[:, y, :, ASIDE:] = jnp.broadcast_to(part[None], (nz,) + part.shape).astype(
            jnp.bfloat16
        )


def aside_of(context, cotangent, weight, inv_tokens, ny, nz):
    rows, cols = weight.shape
    left = cotangent[:, cols // 2 - ASIDE:cols // 2]
    right = cotangent[:, cols - ASIDE:]
    return pl.pallas_call(
        functools.partial(aside_kernel, inv_tokens),
        out_shape=jax.ShapeDtypeStruct(
            (nz, ny, 4 * rows, ASIDE + cols // (4 * ny)), jnp.bfloat16
        ),
        in_specs=[VMEM] * 4,
        out_specs=VMEM,
        scratch_shapes=[pltpu.VMEM((nz, ny, 2 * rows, ASIDE), jnp.float32)],
        compiler_params=PARAMS,
        name="aside",
    )(context, left, right, weight)


def arrival_kernel(value_ref, sum_ref, weight_ref):
    nz, ny, lines, width = value_ref.shape
    rows = lines // 4
    size = width - ASIDE
    total = value_ref[0, :, :, :ASIDE].astype(jnp.float32)
    for z in range(1, nz):
        total = total + value_ref[z, :, :, :ASIDE].astype(jnp.float32)
    sum_ref[...] = total[:, :2 * rows] + total[:, 2 * rows:]
    for y in range(ny):
        part = value_ref[:, y, :, ASIDE:].astype(jnp.float32)
        for q in range(4):
            start = (y * 4 + q) * size
            block = part[:, q * rows:(q + 1) * rows].reshape(nz * rows, size)
            weight_ref[:, start:start + size] = block.astype(jnp.bfloat16)


def arrival(value):
    nz, ny, lines, width = value.shape
    return pl.pallas_call(
        arrival_kernel,
        out_shape=(
            jax.ShapeDtypeStruct((ny, lines // 2, ASIDE), jnp.float32),
            jax.ShapeDtypeStruct((nz * lines // 4, 4 * ny * (width - ASIDE)), jnp.bfloat16),
        ),
        in_specs=[VMEM],
        out_specs=(VMEM,) * 2,
        compiler_params=PARAMS,
        name="arrival",
    )(value)


def sums_kernel(pieces_ref, aside_ref, state_ref, grad_ref, row_ref, packed_ref):
    grad = jnp.concatenate(
        [jnp.sum(pieces_ref[...], axis=0), jnp.sum(aside_ref[...], axis=0)], axis=1
    )
    grad_ref[...] = grad
    peers, _, size = packed_ref.shape
    lines = size // LANES - 1
    state_sum = jnp.sum(state_ref[...], axis=0, keepdims=True).reshape(1, 1, 1)
    packed_ref[:, :, lines * LANES:] = jnp.broadcast_to(state_sum, (peers, 1, LANES))
    rows = grad.shape[0] // 2
    plain = grad * grad
    squared = plain + EPS1
    row_sum = jnp.sum(squared, axis=1, keepdims=True)
    row_new = BETA * state_ref[...] + (1.0 - BETA) * (row_sum[:rows] + row_sum[rows:])
    row_ref[...] = row_new
    ratio = plain * (1.0 / jnp.concatenate([row_new, row_new], axis=0))
    per_half = grad.shape[1] // LANES
    for which, value in enumerate((squared, ratio)):
        for half in range(2):
            total = jnp.sum(value[half * rows:(half + 1) * rows], axis=0, keepdims=True)
            for i in range(per_half):
                place = (2 * which + half) * per_half + i
                group, line = divmod(place, lines)
                packed_ref[group, :, line * LANES:(line + 1) * LANES] = total[:, i * LANES:(i + 1) * LANES]


def sums_of(pieces, aside, row_state, peers):
    rows, cols = pieces.shape[1], pieces.shape[2] + ASIDE
    return pl.pallas_call(
        sums_kernel,
        out_shape=(
            jax.ShapeDtypeStruct((rows, cols), jnp.float32),
            jax.ShapeDtypeStruct(row_state.shape, jnp.float32),
            jax.ShapeDtypeStruct((peers, 1, 4 * cols // peers + LANES), jnp.float32),
        ),
        in_specs=[VMEM] * 3,
        out_specs=(VMEM,) * 3,
        compiler_params=PARAMS,
        name="sums",
    )(pieces, aside, row_state)


def update_kernel(entries, sums_ref, total_ref, grad_ref, row_ref, state_ref, out_ref, col_ref, rms_ref):
    groups = col_ref.shape[0]
    total = jnp.sum(jnp.sum(sums_ref[:groups], axis=0, keepdims=True), axis=1, keepdims=True)
    total = BETA * total_ref[:1, :1] + (1.0 - BETA) * total
    col_new = BETA * state_ref[...] + (1.0 - BETA) * sums_ref[:groups]
    col_ref[...] = col_new
    ratio = sums_ref[groups:] / col_new
    ratio = jnp.sum(jnp.sum(ratio, axis=0, keepdims=True), axis=1, keepdims=True)
    rms = jnp.sqrt(total * ratio / entries)
    rms_ref[...] = rms
    clip = jnp.maximum(CLIP, rms)
    rows = row_ref.shape[0]
    row = row_ref[...]
    for i in range(groups):
        half, start = divmod(i, groups // 2)
        start *= LANES
        grad = grad_ref[half * rows:(half + 1) * rows, start:start + LANES]
        scaled = grad / jnp.sqrt(row * col_new[i:i + 1] / total)
        out_ref[:, i * LANES:(i + 1) * LANES] = scaled / clip


def update_of(sums, total, grad, row_new, state, entries):
    rows, cols = row_new.shape[0], 2 * grad.shape[1]
    return pl.pallas_call(
        functools.partial(update_kernel, entries),
        out_shape=(
            jax.ShapeDtypeStruct((rows, cols), jnp.float32),
            jax.ShapeDtypeStruct(state.shape, jnp.float32),
            jax.ShapeDtypeStruct((1, 1), jnp.float32),
        ),
        in_specs=[VMEM] * 5,
        out_specs=(VMEM,) * 3,
        compiler_params=PARAMS,
        name="update",
    )(sums, total, grad, row_new, state)


def fold_kernel(value_ref, out_ref):
    total = jnp.sum(value_ref[...], axis=0, keepdims=True)
    out_ref[...] = jnp.broadcast_to(total, out_ref.shape)


def fold(value, copies):
    return pl.pallas_call(
        fold_kernel,
        out_shape=jax.ShapeDtypeStruct((copies,) + value.shape[1:], value.dtype),
        in_specs=[VMEM],
        out_specs=VMEM,
        compiler_params=PARAMS,
        name="fold",
    )(value)


def split_kernel(value_ref, out_ref, last_ref):
    total = jnp.sum(value_ref[...], axis=0, keepdims=True)
    size = out_ref.shape[2]
    out_ref[...] = jnp.broadcast_to(total[:, :, :size], out_ref.shape)
    last_ref[...] = total[0, :, size:]


def split_fold(value, copies):
    size = value.shape[2] - LANES
    return pl.pallas_call(
        split_kernel,
        out_shape=(
            jax.ShapeDtypeStruct((copies, 1, size), value.dtype),
            jax.ShapeDtypeStruct((1, LANES), value.dtype),
        ),
        in_specs=[VMEM],
        out_specs=(VMEM,) * 2,
        compiler_params=PARAMS,
        name="split_fold",
    )(value)


def exchange(value, axes):
    return lax.all_to_all(value, axes, 0, 0, tiled=True)


def on_device(context, cotangent, master_weight, row_state, col_state):
    ny, nz = lax.axis_size("y"), lax.axis_size("z")
    nmp = lax.axis_size("x") * lax.axis_size("c")
    rows, cols = master_weight.shape
    inv_tokens = 1.0 / (cotangent.shape[0] * ny * nz)
    entries = rows * ny * nz * nmp * cols

    term = term_of(context, cotangent, inv_tokens, ny * nz, rows)
    part = lax.psum_scatter(
        term.reshape(ny * nz * 2 * rows, term.shape[2]), "y", scatter_dimension=0, tiled=True
    )
    context, _ = lax.optimization_barrier((context, term))
    aside = aside_of(context, cotangent, master_weight, inv_tokens, ny, nz)
    aside, weight_rows = arrival(exchange(aside, "z"))
    aside = exchange(aside, "y")
    weight_rows, part, aside = lax.optimization_barrier((weight_rows, part, aside))
    weight = lax.all_gather(weight_rows, "y", axis=0, tiled=True)
    grad_input = lax.dot_general(
        cotangent, weight, (((1,), (1,)), ((), ())), preferred_element_type=jnp.float32
    ).astype(jnp.bfloat16)

    pieces = exchange(part.reshape(nz, 2 * rows, term.shape[2]), "z")
    grad, row_new, packed = sums_of(pieces, aside, row_state[:, None], nmp)
    packed = fold(exchange(packed, NEAR), ny * nz)
    packed, state_sum = split_fold(exchange(packed, FAR), nmp)
    packed = exchange(packed, NEAR).reshape(2 * cols // LANES, LANES)
    packed, grad_input = lax.optimization_barrier((packed, grad_input))
    update, col_new, update_rms = update_of(
        packed, state_sum, grad, row_new, col_state.reshape(cols // LANES, LANES), entries
    )
    return (grad_input, update, row_new[:, 0], col_new.reshape(cols), update_rms[0, 0])


def solution(mesh):
    grid = Mesh(mesh.devices.reshape(8, 8, 4, 2), ("y", "z", "x", "c"))
    dp, mp = ("y", "z"), ("x", "c")
    in_specs = (P(dp, mp), P(dp, None), P(mp + dp, None), P(mp + dp), P())
    out_specs = (P(dp, mp), P(mp + dp, None), P(mp + dp), P(), P())
    return jax.shard_map(
        on_device, mesh=grid, in_specs=in_specs, out_specs=out_specs, check_vma=False
    )
```
